512 devices in a mesh: cell: 32 (over z, x), gene: 16 (over y, core).
Axes of the slice: x: 4, y: 8, z: 8, core: 2. Of those that a mesh axis runs over, the one named last changes fastest.
Arguments:
- block_values: bfloat16 [32, 16, 96, 128, 128], P('cell', 'gene'), may hold values from -6 to 6, as said below
- block_ids: int32 [32, 16, 96], P('cell', 'gene'), may hold values from 0 to 119, as said below
- block_count: int32 [32, 16], P('cell', 'gene'), may hold values from 12 to 96, as said below
- cell_factor: bfloat16 [16384, 128], P('cell'), may hold values from -6 to 6
- gene_factor: bfloat16 [61440, 128], P('gene'), may hold values from -1.796875 to 1.796875
Outputs:
- new_cells: bfloat16 [16384, 128], P('cell')
- new_genes: bfloat16 [61440, 128], P('gene')
The draws below stay inside these ranges and needn't reach their ends.
Inputs may be any that keep to these rules, and one draw needn't show every extreme that they name: `block_ids`: within one device's list the 96 entries are distinct. Only the first block_count slots of a device's list are live; the values of the other slots are not used. Some device has all 96 slots live. `block_values`: about four entries in ten are zero.
All inputs are finite; a program needn't handle non-finite values.
Results may differ from the reference program's by a relative error of at most 0.012.
Values may be sent and summed in bfloat16 or wider, within the bound.
No kernel may reach another device: no remote copies, remote signals or barrier semaphores. Data moves between devices by JAX's collectives and lax.ppermute only.
A program may use at most 64 MiB of HBM per device.

```python
import jax
import jax.numpy as jnp
from jax import lax

RANK = 128
BLK = 128
GENES = 61440
CB_DEV = 4
NB_MAX = 96
GB_DEV = 30
CELLS = 16384
N_CELL = 32
N_GENE = 16


def draw_block_values(key, part):
    key = jax.random.fold_in(key, 11)
    key_values, key_zeros = jax.random.split(key, 2)
    shape = (N_CELL, N_GENE, NB_MAX, BLK, BLK)
    base = jnp.clip(jax.random.normal(key_values, shape, jnp.float32), -6.0, 6.0)
    keep = jax.random.bernoulli(key_zeros, 0.6, shape)
    return jnp.where(keep, base, 0.0).astype(jnp.bfloat16)


def draw_block_ids(key, part):
    key = jax.random.fold_in(key, 23)
    keys = jax.random.split(key, N_CELL * N_GENE)
    orders = jax.vmap(lambda single: jax.random.permutation(single, CB_DEV * GB_DEV))(keys)
    return orders[:, :NB_MAX].reshape(N_CELL, N_GENE, NB_MAX).astype(jnp.int32)


def draw_block_count(key, part):
    key = jax.random.fold_in(key, 37)
    key_level, key_full = jax.random.split(key)
    lowest = NB_MAX // 8
    levels = jax.random.randint(key_level, (N_CELL * N_GENE,), 0, 65, dtype=jnp.int32)
    counts = lowest + levels * levels * (NB_MAX - lowest) // 4096
    chosen = jax.random.randint(key_full, (), 0, N_CELL * N_GENE, dtype=jnp.int32)
    counts = counts.at[chosen].set(NB_MAX)
    return counts.reshape(N_CELL, N_GENE).astype(jnp.int32)


def shard_levels(rng, shape, pieces, low, top_value):
    def one(position, blocks):
        draws = jax.random.uniform(jax.random.fold_in(jax.random.fold_in(rng, 6), position), (blocks,), jnp.float32, low / len(pieces), top_value / len(pieces))
        return jnp.repeat(jnp.exp(draws), shape[position] // blocks).reshape((-1,) + (1,) * (len(shape) - position - 1))

    gain = one(*pieces[0])
    for cut in pieces[1:]:
        gain = gain * one(*cut)
    return gain


def noise(key, shape, deviation, most, cuts=(), kind=jnp.bfloat16):
    drawn = jax.random.normal(key, shape, jnp.float32) * deviation
    if len(cuts) > 0:
        drawn = shard_levels(key, shape, cuts, -0.22, 0.18) * drawn
    return jnp.clip(drawn, min=-most, max=most).astype(kind)


def setup_inputs(seed: int = 0) -> dict:
    splits = jax.random.split(jax.random.key(seed), 6)
    block_values = draw_block_values(jax.random.fold_in(splits[5], 71), 0)
    block_ids = draw_block_ids(jax.random.fold_in(splits[5], 71), 0)
    block_count = draw_block_count(jax.random.fold_in(splits[5], 71), 0)
    cell_factor = noise(splits[3], (CELLS, RANK), 1.0, 6.0, ((0, 32),))
    gene_factor = noise(splits[4], (GENES, RANK), 0.3, 1.796875, ((0, 16),))
    return {"block_values": block_values, "block_ids": block_ids, "block_count": block_count, "cell_factor": cell_factor, "gene_factor": gene_factor}


LAMBDA = 0.5

def solve_right(matrix, gram):
    eye = jnp.eye(gram.shape[0], dtype=jnp.float32)
    lower_factor = jnp.linalg.cholesky(gram + LAMBDA * eye)
    middle = lax.linalg.triangular_solve(lower_factor, matrix, left_side=False, lower=True, transpose_a=True)
    return lax.linalg.triangular_solve(lower_factor, middle, left_side=False, lower=True, transpose_a=False)

def tile_resid(values, ids, count, cell_tiles, gene_tiles, scale):
    rows = ids // GB_DEV
    cols = ids % GB_DEV
    cell_blocks = cell_tiles[rows].astype(jnp.float32)
    gene_blocks = gene_tiles[cols].astype(jnp.float32)
    fitted = scale * jnp.einsum('nir,njr->nij', cell_blocks, gene_blocks)
    slots = jnp.arange(NB_MAX, dtype=jnp.int32)
    keep = (slots < count)[:, None, None] & (values != 0)
    resid = jnp.where(keep, values.astype(jnp.float32) - fitted, 0.0).astype(jnp.bfloat16)
    return (resid, cell_blocks, gene_blocks, rows, cols)

def reference(block_values, block_ids, block_count, cell_factor, gene_factor):
    scale = CELLS ** (-0.5)
    gram_cells = scale * scale * jnp.dot(cell_factor.T.astype(jnp.float32), cell_factor.astype(jnp.float32), preferred_element_type=jnp.float32)
    cell_all = cell_factor.reshape(N_CELL, CB_DEV, BLK, RANK)
    gene_all = gene_factor.reshape(N_GENE, GB_DEV, BLK, RANK)
    gene_range = jnp.arange(GB_DEV, dtype=jnp.int32)
    cell_range = jnp.arange(CB_DEV, dtype=jnp.int32)

    def gene_step(total, cell_index):

        def per_tile(gene_index):
            resid, cell_blocks, gene_blocks, rows, cols = tile_resid(block_values[cell_index, gene_index], block_ids[cell_index, gene_index], block_count[cell_index, gene_index], cell_all[cell_index], gene_all[gene_index], scale)
            terms = jnp.einsum('nij,nir->njr', resid.astype(jnp.float32), cell_blocks)
            onehot = (cols[None, :] == gene_range[:, None]).astype(jnp.float32)
            return scale * jnp.einsum('gn,njr->gjr', onehot, terms, precision=lax.Precision.HIGHEST)
        parts = lax.map(per_tile, jnp.arange(N_GENE, dtype=jnp.int32))
        return (total + parts.reshape(GENES, RANK), None)
    gene_terms, unused = lax.scan(gene_step, jnp.zeros((GENES, RANK), jnp.float32), jnp.arange(N_CELL, dtype=jnp.int32))
    right_side = gene_terms + jnp.dot(gene_factor.astype(jnp.float32), gram_cells, precision=lax.Precision.HIGHEST)
    new_genes = solve_right(right_side, gram_cells).astype(jnp.bfloat16)
    gram_genes = jnp.dot(new_genes.T.astype(jnp.float32), new_genes.astype(jnp.float32), preferred_element_type=jnp.float32)
    new_all = new_genes.reshape(N_GENE, GB_DEV, BLK, RANK)

    def cell_step(carry, cell_index):

        def per_tile(gene_index):
            resid, cell_blocks, gene_blocks, rows, cols = tile_resid(block_values[cell_index, gene_index], block_ids[cell_index, gene_index], block_count[cell_index, gene_index], cell_all[cell_index], new_all[gene_index], scale)
            terms = jnp.einsum('nij,njr->nir', resid.astype(jnp.float32), gene_blocks)
            onehot = (rows[None, :] == cell_range[:, None]).astype(jnp.float32)
            return jnp.einsum('cn,nir->cir', onehot, terms, precision=lax.Precision.HIGHEST)
        parts = lax.map(per_tile, jnp.arange(N_GENE, dtype=jnp.int32))
        return (carry, jnp.sum(parts, axis=0).reshape(CB_DEV * BLK, RANK))
    unused, cell_parts = lax.scan(cell_step, jnp.zeros((), jnp.float32), jnp.arange(N_CELL, dtype=jnp.int32))
    cell_terms = cell_parts.reshape(CELLS, RANK)
    right_cells = cell_terms + scale * jnp.dot(cell_factor.astype(jnp.float32), gram_genes, precision=lax.Precision.HIGHEST)
    new_cells = (solve_right(right_cells, gram_genes) / scale).astype(jnp.bfloat16)
    return (new_cells, new_genes)
```

```python
import functools

import jax
import jax.numpy as jnp
from jax import lax
from jax.experimental import pallas as pl
from jax.experimental.pallas import tpu as pltpu
from jax.sharding import PartitionSpec as P

LAMBDA = 0.5
F32 = jnp.float32
BF16 = jnp.bfloat16
NN = (((1,), (0,)), ((), ()))
NT = (((1,), (1,)), ((), ()))
TN = (((0,), (0,)), ((), ()))
VMEM_LIMIT = 40 * 1024 * 1024


def dot(a, b, dims=NN):
    return lax.dot_general(a, b, dims, preferred_element_type=F32)


def split(value):
    high = value.astype(BF16)
    return high, (value - high.astype(F32)).astype(BF16)


def fill_positions(ids_ref, count_ref, pos_ref):
    slots = ids_ref.shape[0]

    def clear(i, carry):
        pos_ref[i] = slots
        return carry

    lax.fori_loop(0, pos_ref.shape[0], clear, 0, unroll=8)

    def place(k, carry):
        pos_ref[ids_ref[k]] = k
        return carry

    lax.fori_loop(0, count_ref[0], place, 0)


def residual_pair(vals_ref, pos_ref, resid_ref, cells_ref, genes, first, gene_blocks):
    slots, blk, _ = vals_ref.shape
    for c in range(cells_ref.shape[0] // blk):
        rows = pl.ds(c * blk, blk)
        fit = dot(cells_ref[rows, :], genes, NT)
        for h in range(2):
            slot = pos_ref[c * gene_blocks + first + h]
            live = (slot < slots).astype(F32)
            value = vals_ref[jnp.minimum(slot, slots - 1)].astype(F32) * live
            part = value - fit[:, h * blk : (h + 1) * blk]
            resid_ref[rows, h * blk : (h + 1) * blk] = jnp.where(value != 0.0, part, 0.0).astype(BF16)


def first_pass_kernel(
    start, blocks, scale, gene_blocks, ids_ref, count_ref, vals_ref, cell_ref, gene_ref, out_ref, pos_ref, cells_ref, turned_ref, resid_ref
):
    blk = vals_ref.shape[1]
    fill_positions(ids_ref, count_ref, pos_ref)
    scaled = cell_ref[...].astype(F32) * scale
    cells_ref[...] = scaled.astype(BF16)
    turned_ref[...] = scaled.T.astype(BF16)

    def step(p, carry):
        first = start + 2 * p
        genes = gene_ref[pl.ds(pl.multiple_of(first * blk, blk), 2 * blk), :]
        residual_pair(vals_ref, pos_ref, resid_ref, cells_ref, genes, first, gene_blocks)
        terms = dot(turned_ref[...], resid_ref[...]).astype(BF16)
        out_ref[2 * p] = terms[:, :blk]
        out_ref[2 * p + 1] = terms[:, blk:]
        return carry

    lax.fori_loop(0, blocks // 2, step, 0)


def first_pass(start, blocks, scale, gene_blocks, ids, count, values, cells, genes):
    blk = values.shape[1]
    rows, rank = cells.shape
    smem = pl.BlockSpec(memory_space=pltpu.SMEM)
    vmem = pl.BlockSpec(memory_space=pltpu.VMEM)
    return pl.pallas_call(
        functools.partial(first_pass_kernel, start, blocks, scale, gene_blocks),
        out_shape=jax.ShapeDtypeStruct((blocks, rank, blk), BF16),
        in_specs=[smem, smem, vmem, vmem, vmem],
        out_specs=vmem,
        scratch_shapes=[
            pltpu.SMEM((rows // blk * gene_blocks,), jnp.int32),
            pltpu.VMEM((rows, rank), BF16),
            pltpu.VMEM((rank, rows), BF16),
            pltpu.VMEM((rows, 2 * blk), BF16),
        ],
        compiler_params=pltpu.CompilerParams(vmem_limit_bytes=VMEM_LIMIT),
        name="first_pass",
    )(ids, count, values, cells, genes)


def second_pass_kernel(
    start, blocks, scale, gene_blocks, ids_ref, count_ref, vals_ref, cell_ref, new_ref, sum_ref, out_ref, pos_ref, cells_ref, resid_ref, total_ref
):
    blk = vals_ref.shape[1]
    fill_positions(ids_ref, count_ref, pos_ref)
    cells_ref[...] = (cell_ref[...].astype(F32) * scale).astype(BF16)
    total_ref[...] = sum_ref[...].astype(F32)

    def step(p, carry):
        first = start + 2 * p
        genes = new_ref[pl.ds(pl.multiple_of(2 * p * blk, blk), 2 * blk), :]
        residual_pair(vals_ref, pos_ref, resid_ref, cells_ref, genes, first, gene_blocks)
        total_ref[...] += dot(resid_ref[...], genes)
        return carry

    lax.fori_loop(0, blocks // 2, step, 0)
    out_ref[...] = total_ref[...].astype(out_ref.dtype)


def second_pass(start, blocks, scale, gene_blocks, ids, count, values, cells, new, total, kind):
    blk = values.shape[1]
    rows, rank = cells.shape
    smem = pl.BlockSpec(memory_space=pltpu.SMEM)
    vmem = pl.BlockSpec(memory_space=pltpu.VMEM)
    return pl.pallas_call(
        functools.partial(second_pass_kernel, start, blocks, scale, gene_blocks),
        out_shape=jax.ShapeDtypeStruct((rows, rank), kind),
        in_specs=[smem, smem, vmem, vmem, vmem, vmem],
        out_specs=vmem,
        scratch_shapes=[
            pltpu.SMEM((rows // blk * gene_blocks,), jnp.int32),
            pltpu.VMEM((rows, rank), BF16),
            pltpu.VMEM((rows, 2 * blk), BF16),
            pltpu.VMEM((rows, rank), F32),
        ],
        compiler_params=pltpu.CompilerParams(vmem_limit_bytes=VMEM_LIMIT),
        name="second_pass",
    )(ids, count, values, cells, new, total)


def new_genes_kernel(solve_ref, gene_ref, sums_ref, gram_in_ref, new_ref, gram_ref):
    blk = sums_ref.shape[1]
    blocks = sums_ref.shape[0]
    rank = solve_ref.shape[0]
    gram_ref[...] = gram_in_ref[...]

    def step(p, carry):
        rows = pl.ds(pl.multiple_of(2 * p * blk, blk), 2 * blk)
        genes = gene_ref[rows, :]
        sums = jnp.concatenate([sums_ref[2 * p], sums_ref[2 * p + 1]], axis=1)
        turned = (
            dot(solve_ref[:, 0:rank], genes, NT)
            + dot(solve_ref[:, rank : 2 * rank], genes, NT)
            + dot(solve_ref[:, 2 * rank : 3 * rank], sums)
            + dot(solve_ref[:, 3 * rank : 4 * rank], sums)
        )
        low = turned.astype(BF16)
        new = turned.T.astype(BF16)
        new_ref[rows, :] = new
        gram_ref[...] += dot(low, new)
        return carry

    lax.fori_loop(0, blocks // 2, step, 0)


def make_new_genes(solve, genes, sums, gram):
    vmem = pl.BlockSpec(memory_space=pltpu.VMEM)
    rows = sums.shape[0] * sums.shape[1]
    rank = gram.shape[0]
    return pl.pallas_call(
        new_genes_kernel,
        out_shape=(jax.ShapeDtypeStruct((rows, rank), BF16), jax.ShapeDtypeStruct((rank, rank), F32)),
        in_specs=[vmem] * 4,
        out_specs=(vmem, vmem),
        compiler_params=pltpu.CompilerParams(vmem_limit_bytes=VMEM_LIMIT),
        name="new_genes",
    )(solve, genes, sums, gram)


def inverse_kernel(parts_ref, out_ref):
    rank = out_ref.shape[0]
    gram = parts_ref[0].astype(F32)
    for part in range(1, parts_ref.shape[0]):
        gram = gram + parts_ref[part].astype(F32)
    row = lax.broadcasted_iota(jnp.int32, (rank, rank), 0)
    column = lax.broadcasted_iota(jnp.int32, (rank, rank), 1)
    work = gram + jnp.where(row == column, LAMBDA, 0.0)
    for k in range(rank):
        at_row = row[:, 0:1] == k
        at_column = column[0:1, :] == k
        line = work[k : k + 1, :]
        pivot = 1.0 / work[k : k + 1, k : k + 1]
        side = work[:, k : k + 1] - jnp.where(at_row, 1.0, 0.0)
        line = jnp.where(at_column, 1.0, line) * pivot
        kept = jnp.where(at_column, jnp.where(at_row, 1.0, 0.0), work)
        work = kept - side * line
    product = lax.dot_general(gram, work, NN, precision=lax.Precision.HIGHEST, preferred_element_type=F32)
    high, low = split(product)
    out_ref[:, 0:rank] = high.T
    out_ref[:, rank : 2 * rank] = low.T
    high, low = split(work)
    out_ref[:, 2 * rank : 3 * rank] = high
    out_ref[:, 3 * rank : 4 * rank] = low


def inverse(parts):
    vmem = pl.BlockSpec(memory_space=pltpu.VMEM)
    rank = parts.shape[-1]
    return pl.pallas_call(
        inverse_kernel,
        out_shape=jax.ShapeDtypeStruct((rank, 4 * rank), BF16),
        in_specs=[vmem],
        out_specs=vmem,
        compiler_params=pltpu.CompilerParams(vmem_limit_bytes=VMEM_LIMIT),
        name="inverse",
    )(parts)


def new_cells_kernel(scale, solve_ref, cell_ref, sums_ref, out_ref):
    rank = cell_ref.shape[1]
    sums = (sums_ref[...].astype(F32) * (1.0 / scale)).astype(BF16)
    out_ref[...] = (
        dot(cell_ref[...], solve_ref[:, 0:rank], NT)
        + dot(cell_ref[...], solve_ref[:, rank : 2 * rank], NT)
        + dot(sums, solve_ref[:, 2 * rank : 3 * rank], NT)
        + dot(sums, solve_ref[:, 3 * rank : 4 * rank], NT)
    ).astype(BF16)


def make_new_cells(scale, solve, cells, sums):
    vmem = pl.BlockSpec(memory_space=pltpu.VMEM)
    return pl.pallas_call(
        functools.partial(new_cells_kernel, scale),
        out_shape=jax.ShapeDtypeStruct(cells.shape, BF16),
        in_specs=[vmem] * 3,
        out_specs=vmem,
        compiler_params=pltpu.CompilerParams(vmem_limit_bytes=VMEM_LIMIT),
        name="new_cells",
    )(solve, cells, sums)


def exchange(parts, axes):
    return lax.all_to_all(parts, axes, 0, 0, tiled=True)


def spread(part, axes):
    return exchange(jnp.broadcast_to(part[None], (lax.axis_size(axes),) + part.shape), axes)


def body(block_values, block_ids, block_count, cell_factor, gene_factor):
    values = block_values[0, 0]
    ids = block_ids[0, 0]
    count = block_count[0]
    blk = values.shape[1]
    rows, rank = cell_factor.shape
    gene_blocks = gene_factor.shape[0] // blk
    n_cell, n_gene = lax.axis_size("cell"), lax.axis_size("gene")
    scale = (rows * n_cell) ** (-0.5)
    share = rank // n_gene

    scaled = (cell_factor.astype(F32) * scale).astype(BF16)
    mine = lax.dynamic_slice_in_dim(scaled, lax.axis_index("gene") * share, share, 1)
    gram_rows = lax.dot_general(mine, scaled, TN, preferred_element_type=F32).astype(BF16)

    terms = first_pass(0, gene_blocks, scale, gene_blocks, ids, count, values, cell_factor, gene_factor)
    terms = terms.reshape(n_cell, -1, blk)
    height = terms.shape[1]
    message = jnp.concatenate([terms, jnp.broadcast_to(gram_rows[None], (n_cell, share, rank))], axis=1)
    got = exchange(message, "cell").astype(F32).sum(axis=0)
    gram_cells = spread(got[height:], "gene").reshape(1, rank, rank)
    sums = spread(got[:height].astype(BF16), "cell").reshape(gene_blocks, rank, blk)
    solve_genes = inverse(gram_cells)
    new_genes, gram = make_new_genes(solve_genes, gene_factor, sums, jnp.zeros((rank, rank), F32))
    gram_parts = spread(gram.astype(BF16), "gene")
    cell_terms = second_pass(
        0, gene_blocks, scale, gene_blocks, ids, count, values, cell_factor, new_genes, jnp.zeros((rows, rank), BF16), BF16
    )
    got_cells = exchange(cell_terms.reshape(n_gene, -1, rank), "gene").astype(F32).sum(axis=0).astype(BF16)
    cell_sums = spread(got_cells, "gene").reshape(rows, rank)
    solve_cells = inverse(gram_parts)
    new_cells = make_new_cells(scale, solve_cells, cell_factor, cell_sums)
    return new_cells, new_genes


def solution(mesh):
    return jax.shard_map(
        body,
        mesh=mesh,
        in_specs=(
            P("cell", "gene", None, None, None),
            P("cell", "gene", None),
            P("cell", "gene"),
            P("cell", None),
            P("gene", None),
        ),
        out_specs=(P("cell", None), P("gene", None)),
        check_vma=False,
    )
```

```python
import functools

import jax
import jax.numpy as jnp
from jax import lax
from jax.experimental import pallas as pl
from jax.experimental.pallas import tpu as pltpu
from jax.sharding import PartitionSpec as P

LAMBDA = 0.5
F32 = jnp.float32
BF16 = jnp.bfloat16
NN = (((1,), (0,)), ((), ()))
NT = (((1,), (1,)), ((), ()))
PARAMS = pltpu.CompilerParams(vmem_limit_bytes=48 * 1024 * 1024)
SMEM = pl.BlockSpec(memory_space=pltpu.SMEM)
VMEM = pl.BlockSpec(memory_space=pltpu.VMEM)
HBM = pl.BlockSpec(memory_space=pltpu.HBM)
GROUP = 15
PIECES = 4


def dot(a, b, dims=NN):
    return lax.dot_general(a, b, dims, preferred_element_type=F32)


def exact_dot(a, b):
    return lax.dot_general(a, b, NN, precision=lax.Precision.HIGHEST, preferred_element_type=F32)


def split(value):
    high = value.astype(BF16)
    return high, (value - high.astype(F32)).astype(BF16)


def two_terms(value):
    high = value.astype(BF16).astype(F32)
    return jnp.concatenate([high, value - high], axis=0).astype(BF16)


def start_loads(sem, pairs):
    copies = []
    source, target = pairs[0]
    step = source.shape[0] // PIECES
    for i in range(PIECES):
        part = pl.ds(i * step, step)
        copies.append(pltpu.make_async_copy(source.at[part], target.at[part], sem.at[i]))
    for i, (source, target) in enumerate(pairs[1:]):
        copies.append(pltpu.make_async_copy(source, target, sem.at[PIECES + i]))
    for copy in reversed(copies):
        copy.start()
    return copies[:PIECES], copies[PIECES:]


def fill_positions(ids_ref, count_ref, pos_ref):
    slots = ids_ref.shape[0]
    for i in range(pos_ref.shape[0]):
        pos_ref[i] = slots
    count = count_ref[0]
    for k in range(slots):
        pos_ref[ids_ref[k]] = jnp.where(k < count, k, slots)


def residual_pair(vals_ref, pos_ref, resid_ref, cells_ref, genes, first, gene_blocks, at):
    slots, blk, _ = vals_ref.shape
    for c in range(cells_ref.shape[0] // blk):
        rows = pl.ds(c * blk, blk)
        fit = dot(cells_ref[rows, :], genes, NT)
        for h in range(2):
            slot = pos_ref[c * gene_blocks + first + h]
            live = (slot < slots).astype(F32)
            value = vals_ref[jnp.minimum(slot, slots - 1)].astype(F32) * live
            part = value - fit[:, h * blk : (h + 1) * blk]
            to = pl.ds((at + h) * blk, blk)
            resid_ref[rows, to] = jnp.where(value != 0.0, part, 0.0).astype(BF16)


def first_pass_kernel(
    scale, gene_blocks, ids_ref, count_ref, vals_hbm, cell_hbm, gene_hbm, out_ref, sem, pos_ref, vals_ref, cell_ref, gene_ref, turned_ref, resid_ref, flat_ref
):
    blk = vals_ref.shape[1]
    owners, height, _ = out_ref.shape
    share = gene_blocks * blk // owners
    values, others = start_loads(sem, [(vals_hbm, vals_ref), (gene_hbm, gene_ref), (cell_hbm, cell_ref)])
    fill_positions(ids_ref, count_ref, pos_ref)
    others[1].wait()
    scaled = cell_ref[...].astype(F32) * scale
    turned_ref[...] = scaled.T.astype(BF16)
    cell_ref[...] = scaled.astype(BF16)
    gram = dot(turned_ref[...], cell_ref[...])
    rows = (height - share) // 2
    for owner in range(owners):
        out_ref[owner, share:, :] = two_terms(gram[owner * rows : (owner + 1) * rows, :])
    others[0].wait()
    for copy in values:
        copy.wait()

    def step(p, carry):
        for u in range(GROUP):
            first = 2 * (p * GROUP + u)
            genes = gene_ref[pl.ds(pl.multiple_of(first * blk, blk), 2 * blk), :]
            residual_pair(vals_ref, pos_ref, resid_ref, cell_ref, genes, first, gene_blocks, 2 * u)
        terms = dot(turned_ref[...], resid_ref[...]).astype(BF16)
        for u in range(2 * GROUP):
            to = pl.ds(pl.multiple_of((2 * p * GROUP + u) * blk, blk), blk)
            flat_ref[to, :] = terms[:, u * blk : (u + 1) * blk]
        return carry

    lax.fori_loop(0, gene_blocks // (2 * GROUP), step, 0)
    for owner in range(owners):
        out_ref[owner, :share, :] = flat_ref[owner * share : (owner + 1) * share, :]


def first_pass(scale, owners, ids, count, values, cells, genes):
    slots, blk, _ = values.shape
    rows, rank = cells.shape
    gene_blocks = genes.shape[0] // blk
    height = genes.shape[0] // owners + 2 * (rank // owners)
    return pl.pallas_call(
        functools.partial(first_pass_kernel, scale, gene_blocks),
        out_shape=jax.ShapeDtypeStruct((owners, height, blk), BF16),
        in_specs=[SMEM, SMEM, HBM, HBM, HBM],
        out_specs=VMEM,
        scratch_shapes=[
            pltpu.SemaphoreType.DMA((PIECES + 2,)),
            pltpu.SMEM((rows // blk * gene_blocks,), jnp.int32),
            pltpu.VMEM(values.shape, BF16),
            pltpu.VMEM(cells.shape, BF16),
            pltpu.VMEM(genes.shape, BF16),
            pltpu.VMEM((rank, rows), BF16),
            pltpu.VMEM((rows, 2 * GROUP * blk), BF16),
            pltpu.VMEM(genes.shape, BF16),
        ],
        compiler_params=pltpu.CompilerParams(vmem_limit_bytes=63 * 1024 * 1024),
        name="first_pass",
    )(ids, count, values, cells, genes)


def add_up_kernel(share, parts_ref, out_ref):
    parts, height, _ = parts_ref.shape
    step = share // 4 if share % 32 == 0 else share // 5
    low = 0
    while low < share:
        rows = pl.ds(low, step)
        total = parts_ref[0, rows, :].astype(F32)
        for i in range(1, parts):
            total = total + parts_ref[i, rows, :].astype(F32)
        total = total.astype(BF16)
        for i in range(out_ref.shape[0]):
            out_ref[i, rows, :] = total
        low += step
    rows = pl.ds(share, height - share)
    total = parts_ref[0, rows, :].astype(F32)
    for i in range(1, parts):
        total = total + parts_ref[i, rows, :].astype(F32)
    half = (height - share) // 2
    gram = two_terms(total[:half, :] + total[half:, :])
    for i in range(out_ref.shape[0]):
        out_ref[i, rows, :] = gram


def add_up(share, parts):
    return pl.pallas_call(
        functools.partial(add_up_kernel, share),
        out_shape=jax.ShapeDtypeStruct(parts.shape, BF16),
        in_specs=[VMEM],
        out_specs=VMEM,
        compiler_params=PARAMS,
        name="add_up",
    )(parts)


def eliminate(work, row, column):
    for k in range(work.shape[0]):
        at_row = row[:, 0:1] == k
        at_column = column[0:1, :] == k
        line = work[k : k + 1, :]
        pivot = 1.0 / work[k : k + 1, k : k + 1]
        side = work[:, k : k + 1] - jnp.where(at_row, 1.0, 0.0)
        line = jnp.where(at_column, 1.0, line) * pivot
        kept = jnp.where(at_column, jnp.where(at_row, 1.0, 0.0), work)
        work = kept - side * line
    return work


def solve_into(solve_ref, inverse_ref, gram):
    rank = gram.shape[0]
    row = lax.broadcasted_iota(jnp.int32, (rank, rank), 0)
    column = lax.broadcasted_iota(jnp.int32, (rank, rank), 1)
    diagonal = row == column
    eye = jnp.where(diagonal, 1.0, 0.0)
    matrix = gram + LAMBDA * eye
    along = jnp.where(diagonal, matrix, 0.0)
    down = 1.0 / jnp.sum(along, axis=1, keepdims=True)
    across = 1.0 / jnp.sum(along, axis=0, keepdims=True)
    guess = (eye + (eye - matrix * across)) * down
    for turn in range(3):
        rest = eye - exact_dot(matrix, guess)
        if turn == 2:
            size = jnp.sum(rest * rest)
        guess = guess + dot(guess.astype(BF16), rest.astype(BF16))
    inverse_ref[...] = guess

    @pl.when(jnp.logical_not(size < 1e-6))
    def _():
        inverse_ref[...] = eliminate(matrix, row, column)

    inverse = inverse_ref[...]
    high, low = split(exact_dot(inverse, gram))
    solve_ref[:, 0:rank] = high
    solve_ref[:, rank : 2 * rank] = low
    high, low = split(inverse)
    solve_ref[:, 2 * rank : 3 * rank] = high
    solve_ref[:, 3 * rank : 4 * rank] = low


def second_pass_kernel(
    scale,
    share,
    ids_ref,
    count_ref,
    vals_hbm,
    cell_hbm,
    gene_hbm,
    sums_ref,
    new_hbm,
    out_ref,
    sem,
    out_sem,
    pos_ref,
    vals_ref,
    cell_ref,
    gene_ref,
    flat_ref,
    solve_ref,
    gram_ref,
    new_ref,
    turned_ref,
    resid_ref,
    total_ref,
):
    blk = vals_ref.shape[1]
    rank = cell_ref.shape[1]
    gene_blocks = gene_ref.shape[0] // blk
    senders, height, _ = sums_ref.shape
    values, others = start_loads(sem, [(vals_hbm, vals_ref), (gene_hbm, gene_ref), (cell_hbm, cell_ref)])
    fill_positions(ids_ref, count_ref, pos_ref)
    half = (height - share) // 2
    for i in range(senders):
        flat_ref[i * share : (i + 1) * share, :] = sums_ref[i, :share, :]
        gram = sums_ref[i, share:, :].astype(F32)
        gram_ref[i * half : (i + 1) * half, :] = gram[:half, :] + gram[half:, :]
    solve_into(solve_ref, total_ref.at[:rank, :], gram_ref[...])
    for copy in others + values:
        copy.wait()
    cell_ref[...] = (cell_ref[...].astype(F32) * scale).astype(BF16)
    total_ref[...] = jnp.zeros_like(total_ref)
    width = 2 * GROUP * blk
    steps = gene_blocks // (2 * GROUP)

    def store(p):
        rows = pl.ds(pl.multiple_of(p * width, width), width)
        return pltpu.make_async_copy(new_ref.at[rows], new_hbm.at[rows], out_sem.at[p])

    def step(p, carry):
        for u in range(GROUP):
            first = 2 * (p * GROUP + u)
            base = pl.multiple_of(first * blk, 2 * blk)
            old = gene_ref[pl.ds(base, 2 * blk), :]
            sums = jnp.concatenate([flat_ref[pl.ds(base, blk), :], flat_ref[pl.ds(base + blk, blk), :]], axis=1)
            turned = (
                dot(solve_ref[:, 0:rank], old, NT)
                + dot(solve_ref[:, rank : 2 * rank], old, NT)
                + dot(solve_ref[:, 2 * rank : 4 * rank], jnp.concatenate([sums, sums], axis=0))
            )
            genes = turned.T.astype(BF16)
            turned_ref[:, pl.ds(base, 2 * blk)] = turned.astype(BF16)
            new_ref[pl.ds(base, 2 * blk), :] = genes
            residual_pair(vals_ref, pos_ref, resid_ref, cell_ref, genes, first, gene_blocks, 2 * u)
        total_ref[...] += dot(resid_ref[...], new_ref[pl.ds(pl.multiple_of(p * width, width), width), :])
        store(p).start()
        return carry

    lax.fori_loop(0, steps, step, 0)
    gram = dot(turned_ref[...], new_ref[...])
    owners, out_height, _ = out_ref.shape
    count = total_ref.shape[0] // owners
    half = (out_height - count) // 2
    for i in range(owners):
        out_ref[i, :count, :] = total_ref[i * count : (i + 1) * count, :].astype(BF16)
        out_ref[i, count:, :] = two_terms(gram[i * half : (i + 1) * half, :])

    def finish(p, carry):
        store(p).wait()
        return carry

    lax.fori_loop(0, steps, finish, 0)


def second_pass(scale, share, owners, ids, count, values, cells, genes, sums):
    slots, blk, _ = values.shape
    rows, rank = cells.shape
    gene_blocks = genes.shape[0] // blk
    height = rows // owners + 2 * (rank // owners)
    return pl.pallas_call(
        functools.partial(second_pass_kernel, scale, share),
        out_shape=(jax.ShapeDtypeStruct(genes.shape, BF16), jax.ShapeDtypeStruct((owners, height, rank), BF16)),
        in_specs=[SMEM, SMEM, HBM, HBM, HBM, VMEM],
        out_specs=(HBM, VMEM),
        scratch_shapes=[
            pltpu.SemaphoreType.DMA((PIECES + 2,)),
            pltpu.SemaphoreType.DMA((gene_blocks // (2 * GROUP),)),
            pltpu.SMEM((rows // blk * gene_blocks,), jnp.int32),
            pltpu.VMEM(values.shape, BF16),
            pltpu.VMEM(cells.shape, BF16),
            pltpu.VMEM(genes.shape, BF16),
            pltpu.VMEM(genes.shape, BF16),
            pltpu.VMEM((rank, 4 * rank), BF16),
            pltpu.VMEM((rank, rank), F32),
            pltpu.VMEM(genes.shape, BF16),
            pltpu.VMEM((rank, genes.shape[0]), BF16),
            pltpu.VMEM((rows, 2 * GROUP * blk), BF16),
            pltpu.VMEM((rows, rank), F32),
        ],
        compiler_params=PARAMS,
        name="second_pass",
    )(ids, count, values, cells, genes, sums)


def new_cells_kernel(scale, share, cell_ref, sums_ref, out_ref, solve_ref, gram_ref, inverse_ref):
    rank = cell_ref.shape[1]
    senders, height, _ = sums_ref.shape
    half = (height - share) // 2
    for i in range(senders):
        gram = sums_ref[i, share:, :].astype(F32)
        gram_ref[i * half : (i + 1) * half, :] = gram[:half, :] + gram[half:, :]
    solve_into(solve_ref, inverse_ref, gram_ref[...])
    sums = (sums_ref[:, :share, :].reshape(senders * share, rank).astype(F32) * (1.0 / scale)).astype(BF16)
    out_ref[...] = (
        dot(cell_ref[...], solve_ref[:, 0:rank], NT)
        + dot(cell_ref[...], solve_ref[:, rank : 2 * rank], NT)
        + dot(sums, solve_ref[:, 2 * rank : 3 * rank], NT)
        + dot(sums, solve_ref[:, 3 * rank : 4 * rank], NT)
    ).astype(BF16)


def make_new_cells(scale, share, cells, sums):
    rank = cells.shape[1]
    return pl.pallas_call(
        functools.partial(new_cells_kernel, scale, share),
        out_shape=jax.ShapeDtypeStruct(cells.shape, BF16),
        in_specs=[VMEM] * 2,
        out_specs=VMEM,
        scratch_shapes=[
            pltpu.VMEM((rank, 4 * rank), BF16),
            pltpu.VMEM((rank, rank), F32),
            pltpu.VMEM((rank, rank), F32),
        ],
        compiler_params=PARAMS,
        name="new_cells",
    )(cells, sums)


def exchange(parts, axes):
    return lax.all_to_all(parts, axes, 0, 0, tiled=True)


def body(block_values, block_ids, block_count, cell_factor, gene_factor):
    values = block_values[0, 0]
    ids = block_ids[0, 0]
    count = block_count[0]
    rows = cell_factor.shape[0]
    n_cell, n_gene = lax.axis_size("cell"), lax.axis_size("gene")
    scale = (rows * n_cell) ** (-0.5)
    gene_share = gene_factor.shape[0] // n_cell
    cell_share = rows // n_gene

    terms = first_pass(scale, n_cell, ids, count, values, cell_factor, gene_factor)
    sums = exchange(add_up(gene_share, exchange(terms, "cell")), "cell")
    new_genes, cell_terms = second_pass(scale, gene_share, n_gene, ids, count, values, cell_factor, gene_factor, sums)
    cell_sums = exchange(add_up(cell_share, exchange(cell_terms, "gene")), "gene")
    new_cells = make_new_cells(scale, cell_share, cell_factor, cell_sums)
    return new_cells, new_genes


def solution(mesh):
    return jax.shard_map(
        body,
        mesh=mesh,
        in_specs=(
            P("cell", "gene", None, None, None),
            P("cell", "gene", None),
            P("cell", "gene"),
            P("cell", None),
            P("gene", None),
        ),
        out_specs=(P("cell", None), P("gene", None)),
        check_vma=False,
    )
```

```python
import functools

import jax
import jax.numpy as jnp
from jax import lax
from jax.experimental import pallas as pl
from jax.experimental.pallas import tpu as pltpu
from jax.sharding import PartitionSpec as P

LAMBDA = 0.5
F32 = jnp.float32
BF16 = jnp.bfloat16
NN = (((1,), (0,)), ((), ()))
NT = (((1,), (1,)), ((), ()))
PARAMS = pltpu.CompilerParams(vmem_limit_bytes=48 * 1024 * 1024)
SMEM = pl.BlockSpec(memory_space=pltpu.SMEM)
VMEM = pl.BlockSpec(memory_space=pltpu.VMEM)
HBM = pl.BlockSpec(memory_space=pltpu.HBM)
GROUP = 15
PIECES = 4
INNER = 4


def dot(a, b, dims=NN):
    return lax.dot_general(a, b, dims, preferred_element_type=F32)


def exact_dot(a, b):
    return lax.dot_general(a, b, NN, precision=lax.Precision.HIGHEST, preferred_element_type=F32)


def split(value):
    high = value.astype(BF16)
    return high, (value - high.astype(F32)).astype(BF16)


def two_terms(value):
    high = value.astype(BF16).astype(F32)
    return jnp.concatenate([high, value - high], axis=0).astype(BF16)


def start_loads(sem, pairs):
    copies = []
    source, target = pairs[0]
    step = source.shape[0] // PIECES
    for i in range(PIECES):
        part = pl.ds(i * step, step)
        copies.append(pltpu.make_async_copy(source.at[part], target.at[part], sem.at[i]))
    for i, (source, target) in enumerate(pairs[1:]):
        copies.append(pltpu.make_async_copy(source, target, sem.at[PIECES + i]))
    for copy in reversed(copies):
        copy.start()
    return copies[:PIECES], copies[PIECES:]


def fill_positions(ids_ref, count_ref, pos_ref):
    slots = ids_ref.shape[0]
    for i in range(pos_ref.shape[0]):
        pos_ref[i] = slots
    count = count_ref[0]
    for k in range(slots):
        pos_ref[ids_ref[k]] = jnp.where(k < count, k, slots)


def residual_pair(vals_ref, pos_ref, resid_ref, cells_ref, genes, first, gene_blocks, at):
    blk = vals_ref.shape[1]
    whole = dot(cells_ref[...], genes, NT)
    for c in range(cells_ref.shape[0] // blk):
        rows = pl.ds(c * blk, blk)
        fit = whole[c * blk : (c + 1) * blk, :]
        for h in range(2):
            value = vals_ref[pos_ref[c * gene_blocks + first + h]].astype(F32)
            part = value - fit[:, h * blk : (h + 1) * blk]
            to = pl.ds((at + h) * blk, blk)
            resid_ref[rows, to] = jnp.where(value != 0.0, part, 0.0).astype(BF16)


def first_pass_kernel(
    scale, gene_blocks, ids_ref, count_ref, vals_hbm, cell_hbm, gene_hbm, out_ref, sem, pos_ref, vals_ref, cell_ref, gene_ref, turned_ref, resid_ref, flat_ref
):
    blk = vals_ref.shape[1]
    owners, height, _ = out_ref.shape
    share = gene_blocks * blk // owners
    values, others = start_loads(sem, [(vals_hbm, vals_ref), (gene_hbm, gene_ref), (cell_hbm, cell_ref)])
    fill_positions(ids_ref, count_ref, pos_ref)
    vals_ref[vals_hbm.shape[0]] = jnp.zeros(vals_ref.shape[1:], BF16)
    others[1].wait()
    scaled = cell_ref[...].astype(F32) * scale
    turned_ref[...] = scaled.T.astype(BF16)
    cell_ref[...] = scaled.astype(BF16)
    gram = dot(turned_ref[...], cell_ref[...])
    rows = (height - share) // 2
    for owner in range(owners):
        out_ref[owner, share:, :] = two_terms(gram[owner * rows : (owner + 1) * rows, :])
    others[0].wait()
    for copy in values:
        copy.wait()

    def step(p, carry):
        for u in range(GROUP):
            first = 2 * (p * GROUP + u)
            genes = gene_ref[pl.ds(pl.multiple_of(first * blk, blk), 2 * blk), :]
            residual_pair(vals_ref, pos_ref, resid_ref, cell_ref, genes, first, gene_blocks, 2 * u)
        terms = dot(turned_ref[...], resid_ref[...]).astype(BF16)
        for u in range(2 * GROUP):
            to = pl.ds(pl.multiple_of((2 * p * GROUP + u) * blk, blk), blk)
            flat_ref[to, :] = terms[:, u * blk : (u + 1) * blk]
        return carry

    lax.fori_loop(0, gene_blocks // (2 * GROUP), step, 0)
    for owner in range(owners):
        out_ref[owner, :share, :] = flat_ref[owner * share : (owner + 1) * share, :]


def first_pass(scale, owners, ids, count, values, cells, genes):
    slots, blk, _ = values.shape
    rows, rank = cells.shape
    gene_blocks = genes.shape[0] // blk
    height = genes.shape[0] // owners + 2 * (rank // owners)
    return pl.pallas_call(
        functools.partial(first_pass_kernel, scale, gene_blocks),
        out_shape=jax.ShapeDtypeStruct((owners, height, blk), BF16),
        in_specs=[SMEM, SMEM, HBM, HBM, HBM],
        out_specs=VMEM,
        scratch_shapes=[
            pltpu.SemaphoreType.DMA((PIECES + 2,)),
            pltpu.SMEM((rows // blk * gene_blocks,), jnp.int32),
            pltpu.VMEM((slots + 1, blk, blk), BF16),
            pltpu.VMEM(cells.shape, BF16),
            pltpu.VMEM(genes.shape, BF16),
            pltpu.VMEM((rank, rows), BF16),
            pltpu.VMEM((rows, 2 * GROUP * blk), BF16),
            pltpu.VMEM(genes.shape, BF16),
        ],
        compiler_params=pltpu.CompilerParams(vmem_limit_bytes=63 * 1024 * 1024),
        name="first_pass",
    )(ids, count, values, cells, genes)


def add_up_kernel(share, parts_ref, out_ref):
    parts, slots, height, _ = parts_ref.shape
    pieces = 4 if share % 32 == 0 else 5
    step = share // pieces
    half = (height - share) // 2
    for slot in range(slots):
        for low in range(0, share + step, step):
            rows = pl.ds(low, step if low < share else height - share)
            total = parts_ref[0, slot, rows, :].astype(F32)
            for i in range(1, parts):
                total = total + parts_ref[i, slot, rows, :].astype(F32)
            if low < share:
                total = total.astype(BF16)
            else:
                total = two_terms(total[:half, :] + total[half:, :])
            for i in range(out_ref.shape[0]):
                out_ref[i, slot, rows, :] = total


def add_up(share, copies, parts):
    return pl.pallas_call(
        functools.partial(add_up_kernel, share),
        out_shape=jax.ShapeDtypeStruct((copies,) + parts.shape[1:], BF16),
        in_specs=[VMEM],
        out_specs=VMEM,
        compiler_params=PARAMS,
        name="add_up",
    )(parts)


def eliminate(work, row, column):
    for k in range(work.shape[0]):
        at_row = row[:, 0:1] == k
        at_column = column[0:1, :] == k
        line = work[k : k + 1, :]
        pivot = 1.0 / work[k : k + 1, k : k + 1]
        side = work[:, k : k + 1] - jnp.where(at_row, 1.0, 0.0)
        line = jnp.where(at_column, 1.0, line) * pivot
        kept = jnp.where(at_column, jnp.where(at_row, 1.0, 0.0), work)
        work = kept - side * line
    return work


def solve_into(solve_ref, inverse_ref, gram):
    rank = gram.shape[0]
    row = lax.broadcasted_iota(jnp.int32, (rank, rank), 0)
    column = lax.broadcasted_iota(jnp.int32, (rank, rank), 1)
    diagonal = row == column
    eye = jnp.where(diagonal, 1.0, 0.0)
    matrix = gram + LAMBDA * eye
    along = jnp.where(diagonal, matrix, 0.0)
    down = 1.0 / jnp.sum(along, axis=1, keepdims=True)
    across = 1.0 / jnp.sum(along, axis=0, keepdims=True)
    guess = (eye + (eye - matrix * across)) * down
    for turn in range(3):
        rest = eye - exact_dot(matrix, guess)
        if turn == 2:
            size = jnp.sum(rest * rest)
        guess = guess + dot(guess.astype(BF16), rest.astype(BF16))
    inverse_ref[...] = guess

    @pl.when(jnp.logical_not(size < 1e-6))
    def _():
        inverse_ref[...] = eliminate(matrix, row, column)

    inverse = inverse_ref[...]
    high, low = split(exact_dot(inverse, gram))
    solve_ref[:, 0:rank] = high
    solve_ref[:, rank : 2 * rank] = low
    high, low = split(inverse)
    solve_ref[:, 2 * rank : 3 * rank] = high
    solve_ref[:, 3 * rank : 4 * rank] = low


def second_pass_kernel(
    scale,
    share,
    ids_ref,
    count_ref,
    vals_hbm,
    cell_hbm,
    gene_hbm,
    sums_ref,
    new_hbm,
    out_ref,
    sem,
    out_sem,
    pos_ref,
    vals_ref,
    cell_ref,
    gene_ref,
    flat_ref,
    solve_ref,
    gram_ref,
    new_ref,
    turned_ref,
    resid_ref,
    total_ref,
):
    blk = vals_ref.shape[1]
    rank = cell_ref.shape[1]
    gene_blocks = gene_ref.shape[0] // blk
    senders, height, _ = sums_ref.shape
    values, others = start_loads(sem, [(vals_hbm, vals_ref), (gene_hbm, gene_ref), (cell_hbm, cell_ref)])
    fill_positions(ids_ref, count_ref, pos_ref)
    vals_ref[vals_hbm.shape[0]] = jnp.zeros(vals_ref.shape[1:], BF16)
    half = (height - share) // 2
    for i in range(senders):
        flat_ref[i * share : (i + 1) * share, :] = sums_ref[i, :share, :]
        gram = sums_ref[i, share:, :].astype(F32)
        gram_ref[i * half : (i + 1) * half, :] = gram[:half, :] + gram[half:, :]
    solve_into(solve_ref, total_ref.at[:rank, :], gram_ref[...])
    for copy in others + values:
        copy.wait()
    cell_ref[...] = (cell_ref[...].astype(F32) * scale).astype(BF16)
    total_ref[...] = jnp.zeros_like(total_ref)
    width = 2 * GROUP * blk
    steps = gene_blocks // (2 * GROUP)

    def store(p):
        rows = pl.ds(pl.multiple_of(p * width, width), width)
        return pltpu.make_async_copy(new_ref.at[rows], new_hbm.at[rows], out_sem.at[p])

    def step(p, carry):
        for u in range(GROUP):
            first = 2 * (p * GROUP + u)
            base = pl.multiple_of(first * blk, 2 * blk)
            old = gene_ref[pl.ds(base, 2 * blk), :]
            sums = jnp.concatenate([flat_ref[pl.ds(base, blk), :], flat_ref[pl.ds(base + blk, blk), :]], axis=1)
            turned = (
                dot(solve_ref[:, 0:rank], old, NT)
                + dot(solve_ref[:, rank : 2 * rank], old, NT)
                + dot(solve_ref[:, 2 * rank : 4 * rank], jnp.concatenate([sums, sums], axis=0))
            )
            genes = turned.T.astype(BF16)
            turned_ref[:, pl.ds(base, 2 * blk)] = turned.astype(BF16)
            new_ref[pl.ds(base, 2 * blk), :] = genes
            residual_pair(vals_ref, pos_ref, resid_ref, cell_ref, genes, first, gene_blocks, 2 * u)
        total_ref[...] += dot(resid_ref[...], new_ref[pl.ds(pl.multiple_of(p * width, width), width), :])
        store(p).start()
        return carry

    lax.fori_loop(0, steps, step, 0)
    gram = dot(turned_ref[...], new_ref[...])
    owners, out_height, _ = out_ref.shape
    count = total_ref.shape[0] // owners
    half = (out_height - count) // 2
    for i in range(owners):
        out_ref[i, :count, :] = total_ref[i * count : (i + 1) * count, :].astype(BF16)
        out_ref[i, count:, :] = two_terms(gram[i * half : (i + 1) * half, :])

    def finish(p, carry):
        store(p).wait()
        return carry

    lax.fori_loop(0, steps, finish, 0)


def second_pass(scale, share, owners, ids, count, values, cells, genes, sums):
    slots, blk, _ = values.shape
    rows, rank = cells.shape
    gene_blocks = genes.shape[0] // blk
    height = rows // owners + 2 * (rank // owners)
    return pl.pallas_call(
        functools.partial(second_pass_kernel, scale, share),
        out_shape=(jax.ShapeDtypeStruct(genes.shape, BF16), jax.ShapeDtypeStruct((owners, height, rank), BF16)),
        in_specs=[SMEM, SMEM, HBM, HBM, HBM, VMEM],
        out_specs=(HBM, VMEM),
        scratch_shapes=[
            pltpu.SemaphoreType.DMA((PIECES + 2,)),
            pltpu.SemaphoreType.DMA((gene_blocks // (2 * GROUP),)),
            pltpu.SMEM((rows // blk * gene_blocks,), jnp.int32),
            pltpu.VMEM((slots + 1, blk, blk), BF16),
            pltpu.VMEM(cells.shape, BF16),
            pltpu.VMEM(genes.shape, BF16),
            pltpu.VMEM(genes.shape, BF16),
            pltpu.VMEM((rank, 4 * rank), BF16),
            pltpu.VMEM((rank, rank), F32),
            pltpu.VMEM(genes.shape, BF16),
            pltpu.VMEM((rank, genes.shape[0]), BF16),
            pltpu.VMEM((rows, 2 * GROUP * blk), BF16),
            pltpu.VMEM((rows, rank), F32),
        ],
        compiler_params=PARAMS,
        name="second_pass",
    )(ids, count, values, cells, genes, sums)


def new_cells_kernel(scale, share, cell_ref, sums_ref, out_ref, solve_ref, gram_ref, inverse_ref):
    rank = cell_ref.shape[1]
    senders, height, _ = sums_ref.shape
    half = (height - share) // 2
    for i in range(senders):
        gram = sums_ref[i, share:, :].astype(F32)
        gram_ref[i * half : (i + 1) * half, :] = gram[:half, :] + gram[half:, :]
    solve_into(solve_ref, inverse_ref, gram_ref[...])
    sums = (sums_ref[:, :share, :].reshape(senders * share, rank).astype(F32) * (1.0 / scale)).astype(BF16)
    out_ref[...] = (
        dot(cell_ref[...], solve_ref[:, 0:rank], NT)
        + dot(cell_ref[...], solve_ref[:, rank : 2 * rank], NT)
        + dot(sums, solve_ref[:, 2 * rank : 3 * rank], NT)
        + dot(sums, solve_ref[:, 3 * rank : 4 * rank], NT)
    ).astype(BF16)


def make_new_cells(scale, share, cells, sums):
    rank = cells.shape[1]
    return pl.pallas_call(
        functools.partial(new_cells_kernel, scale, share),
        out_shape=jax.ShapeDtypeStruct(cells.shape, BF16),
        in_specs=[VMEM] * 2,
        out_specs=VMEM,
        scratch_shapes=[
            pltpu.VMEM((rank, 4 * rank), BF16),
            pltpu.VMEM((rank, rank), F32),
            pltpu.VMEM((rank, rank), F32),
        ],
        compiler_params=PARAMS,
        name="new_cells",
    )(cells, sums)


def exchange(parts, axis, groups=None):
    return lax.all_to_all(parts, axis, 0, 0, tiled=True, axis_index_groups=groups)


def across_cells(share, terms):
    owners, height, width = terms.shape
    outer = owners // INNER
    inner_groups = [[o * INNER + i for i in range(INNER)] for o in range(outer)]
    outer_groups = [[o * INNER + i for o in range(outer)] for i in range(INNER)]
    terms = terms.reshape(INNER, outer, height, width)
    terms = add_up(share, 1, exchange(terms, "cell", inner_groups))[0]
    terms = add_up(share, outer, exchange(terms, "cell", outer_groups)[:, None])[:, 0]
    terms = exchange(terms, "cell", outer_groups)
    terms = exchange(add_up(share, INNER, terms[None]), "cell", inner_groups)
    return terms.reshape(owners, height, width)


def body(block_values, block_ids, block_count, cell_factor, gene_factor):
    values = block_values[0, 0]
    ids = block_ids[0, 0]
    count = block_count[0]
    rows = cell_factor.shape[0]
    n_cell, n_gene = lax.axis_size("cell"), lax.axis_size("gene")
    scale = (rows * n_cell) ** (-0.5)
    gene_share = gene_factor.shape[0] // n_cell
    cell_share = rows // n_gene

    terms = first_pass(scale, n_cell, ids, count, values, cell_factor, gene_factor)
    sums = across_cells(gene_share, terms)
    new_genes, cell_terms = second_pass(scale, gene_share, n_gene, ids, count, values, cell_factor, gene_factor, sums)
    cell_sums = exchange(add_up(cell_share, n_gene, exchange(cell_terms, "gene")[:, None])[:, 0], "gene")
    new_cells = make_new_cells(scale, cell_share, cell_factor, cell_sums)
    return new_cells, new_genes


def solution(mesh):
    return jax.shard_map(
        body,
        mesh=mesh,
        in_specs=(
            P("cell", "gene", None, None, None),
            P("cell", "gene", None),
            P("cell", "gene"),
            P("cell", None),
            P("gene", None),
        ),
        out_specs=(P("cell", None), P("gene", None)),
        check_vma=False,
    )
```

```python
import functools

import jax
import jax.numpy as jnp
from jax import lax
from jax.experimental import pallas as pl
from jax.experimental.pallas import tpu as pltpu
from jax.sharding import PartitionSpec as P

LAMBDA = 0.5
F32 = jnp.float32
BF16 = jnp.bfloat16
NN = (((1,), (0,)), ((), ()))
NT = (((1,), (1,)), ((), ()))
PARAMS = pltpu.CompilerParams(vmem_limit_bytes=48 * 1024 * 1024)
SMEM = pl.BlockSpec(memory_space=pltpu.SMEM)
VMEM = pl.BlockSpec(memory_space=pltpu.VMEM)
HBM = pl.BlockSpec(memory_space=pltpu.HBM)
FIRST_STAGES = (5, 10, 15)
SECOND_STAGES = (15,)
AHEAD = 8
PIECES = 4
INNER = 4


def dot(a, b, dims=NN):
    return lax.dot_general(a, b, dims, preferred_element_type=F32)


def exact_dot(a, b):
    return lax.dot_general(a, b, NN, precision=lax.Precision.HIGHEST, preferred_element_type=F32)


def split(value):
    high = value.astype(BF16)
    return high, (value - high.astype(F32)).astype(BF16)


def two_terms(value):
    high = value.astype(BF16).astype(F32)
    return jnp.concatenate([high, value - high], axis=0).astype(BF16)


def start_loads(sem, small, large):
    copies = [pltpu.make_async_copy(source, target, sem.at[i]) for i, (source, target) in enumerate(small)]
    source, target = large
    step = source.shape[0] // PIECES
    for i in range(PIECES):
        part = pl.ds(i * step, step)
        copies.append(pltpu.make_async_copy(source.at[part], target.at[part], sem.at[len(small) + i]))
    for copy in copies:
        copy.start()
    return copies[: len(small)], copies[len(small) :]


def fill_positions(ids_ref, count_ref, pos_ref):
    slots = ids_ref.shape[0]
    for i in range(pos_ref.shape[0]):
        pos_ref[i] = slots
    count = count_ref[0]
    for k in range(slots):
        pos_ref[ids_ref[k]] = jnp.where(k < count, k, slots)


def residual_pair(vals_ref, pos_ref, resid_ref, fit, first, gene_blocks, at):
    blk = vals_ref.shape[1]
    for c in range(fit.shape[0] // blk):
        for h in range(2):
            value = vals_ref[pos_ref[c * gene_blocks + first + h]].astype(F32)
            part = value - fit[c * blk : (c + 1) * blk, h * blk : (h + 1) * blk]
            to = pl.ds((at + h) * blk, blk)
            resid_ref[pl.ds(c * blk, blk), to] = jnp.where(value != 0.0, part, 0.0).astype(BF16)


def first_pass_kernel(
    scale,
    gene_blocks,
    ids_hbm,
    count_ref,
    vals_hbm,
    cell_hbm,
    gene_hbm,
    out_hbm,
    sem,
    out_sem,
    ids_ref,
    pos_ref,
    vals_ref,
    cell_ref,
    gene_ref,
    turned_ref,
    fit_ref,
    resid_ref,
    out_ref,
):
    blk = vals_ref.shape[1]
    rank = cell_ref.shape[1]
    small, values = start_loads(
        sem, [(ids_hbm, ids_ref), (cell_hbm, cell_ref), (gene_hbm, gene_ref)], (vals_hbm, vals_ref.at[: vals_hbm.shape[0]])
    )
    vals_ref[vals_hbm.shape[0]] = jnp.zeros(vals_ref.shape[1:], BF16)
    small[1].wait()
    scaled = cell_ref[...].astype(F32) * scale
    turned_ref[...] = scaled.T.astype(BF16)
    cell_ref[...] = scaled.astype(BF16)
    gram = dot(turned_ref[...], cell_ref[...])
    out_ref[gene_blocks] = two_terms(gram[: rank // 2, :])
    out_ref[gene_blocks + 1] = two_terms(gram[rank // 2 :, :])
    small[2].wait()

    def fit_of(pair):
        return dot(cell_ref[...], gene_ref[2 * pair * blk : 2 * (pair + 1) * blk, :], NT)

    ahead = fit_ref.shape[0]
    for pair in range(ahead):
        fit_ref[pair] = fit_of(pair)
    small[0].wait()
    fill_positions(ids_ref, count_ref, pos_ref)
    for copy in values:
        copy.wait()

    stores = []
    low = 0
    for high in FIRST_STAGES:
        for pair in range(low, high):
            fit = fit_ref[pair] if pair < ahead else fit_of(pair)
            residual_pair(vals_ref, pos_ref, resid_ref, fit, 2 * pair, gene_blocks, 2 * pair)
        terms = dot(turned_ref[...], resid_ref[:, 2 * low * blk : 2 * high * blk]).astype(BF16)
        for u in range(2 * (high - low)):
            out_ref[2 * low + u] = terms[:, u * blk : (u + 1) * blk]
        to = pl.ds(2 * low, 2 * (high - low) + (2 if high == FIRST_STAGES[-1] else 0))
        stores.append(pltpu.make_async_copy(out_ref.at[to], out_hbm.at[to], out_sem.at[len(stores)]))
        stores[-1].start()
        low = high
    for store in stores:
        store.wait()


def first_pass(scale, ids, count, values, cells, genes):
    slots, blk, _ = values.shape
    rows, rank = cells.shape
    gene_blocks = genes.shape[0] // blk
    return pl.pallas_call(
        functools.partial(first_pass_kernel, scale, gene_blocks),
        out_shape=jax.ShapeDtypeStruct((gene_blocks + 2, rank, blk), BF16),
        in_specs=[HBM, SMEM, HBM, HBM, HBM],
        out_specs=HBM,
        scratch_shapes=[
            pltpu.SemaphoreType.DMA((PIECES + 3,)),
            pltpu.SemaphoreType.DMA((len(FIRST_STAGES),)),
            pltpu.SMEM((slots,), jnp.int32),
            pltpu.SMEM((rows // blk * gene_blocks,), jnp.int32),
            pltpu.VMEM((slots + 1, blk, blk), BF16),
            pltpu.VMEM(cells.shape, BF16),
            pltpu.VMEM(genes.shape, BF16),
            pltpu.VMEM((rank, rows), BF16),
            pltpu.VMEM((AHEAD, rows, 2 * blk), F32),
            pltpu.VMEM((rows, genes.shape[0]), BF16),
            pltpu.VMEM((gene_blocks + 2, rank, blk), BF16),
        ],
        compiler_params=pltpu.CompilerParams(vmem_limit_bytes=63 * 1024 * 1024),
        name="first_pass",
    )(ids, count, values, cells, genes)


def total_of(parts_ref, slot, rows):
    total = parts_ref[0, slot, rows, :].astype(F32)
    for i in range(1, parts_ref.shape[0]):
        total = total + parts_ref[i, slot, rows, :].astype(F32)
    return total


def add_blocks_kernel(stage, gram_from, parts_ref, out_ref):
    parts, slots, height, _ = parts_ref.shape
    place = lax.axis_index("cell")
    outer = lax.axis_size("cell") // INNER
    first = (place % INNER) * outer + (place // INNER if stage else 0)
    step = height // 4
    for slot in range(slots):
        may_be_gram = stage or slot >= gram_from % outer
        if may_be_gram:
            whole = total_of(parts_ref, slot, pl.ds(0, height))
            is_gram = first + slot >= gram_from
            gram = two_terms(whole[: height // 2, :] + whole[height // 2 :, :]).astype(F32)
            whole = jnp.where(is_gram, gram, whole).astype(BF16)
            for i in range(out_ref.shape[0]):
                out_ref[i, slot] = whole
        else:
            for low in range(0, height, step):
                rows = pl.ds(low, step)
                out_ref[0, slot, rows, :] = total_of(parts_ref, slot, rows).astype(BF16)


def add_blocks(stage, copies, gram_from, parts):
    return pl.pallas_call(
        functools.partial(add_blocks_kernel, stage, gram_from),
        out_shape=jax.ShapeDtypeStruct((copies,) + parts.shape[1:], BF16),
        in_specs=[VMEM],
        out_specs=VMEM,
        compiler_params=PARAMS,
        name="add_blocks",
    )(parts)


def repeat_kernel(part_ref, out_ref):
    for slot in range(part_ref.shape[0]):
        block = part_ref[slot]
        for i in range(out_ref.shape[0]):
            out_ref[i, slot] = block


def repeat(copies, part):
    return pl.pallas_call(
        repeat_kernel,
        out_shape=jax.ShapeDtypeStruct((copies,) + part.shape, BF16),
        in_specs=[VMEM],
        out_specs=VMEM,
        compiler_params=PARAMS,
        name="repeat",
    )(part)


def add_cells_kernel(share, parts_ref, out_ref):
    senders, height, _ = parts_ref.shape

    def total(rows):
        value = parts_ref[0, rows, :].astype(F32)
        for i in range(1, senders):
            value = value + parts_ref[i, rows, :].astype(F32)
        return value

    cells = total(pl.ds(0, share)).astype(BF16)
    gram = two_terms(total(pl.ds(share, height - share)))
    for i in range(out_ref.shape[0]):
        out_ref[i, :share, :] = cells
        out_ref[i, share:, :] = gram


def add_cells(share, parts):
    senders, height, rank = parts.shape
    return pl.pallas_call(
        functools.partial(add_cells_kernel, share),
        out_shape=jax.ShapeDtypeStruct((senders, 2 * height - share, rank), BF16),
        in_specs=[VMEM],
        out_specs=VMEM,
        compiler_params=PARAMS,
        name="add_cells",
    )(parts)


def eliminate(work, row, column):
    for k in range(work.shape[0]):
        at_row = row[:, 0:1] == k
        at_column = column[0:1, :] == k
        line = work[k : k + 1, :]
        pivot = 1.0 / work[k : k + 1, k : k + 1]
        side = work[:, k : k + 1] - jnp.where(at_row, 1.0, 0.0)
        line = jnp.where(at_column, 1.0, line) * pivot
        kept = jnp.where(at_column, jnp.where(at_row, 1.0, 0.0), work)
        work = kept - side * line
    return work


def solve_into(solve_ref, inverse_ref, gram):
    rank = gram.shape[0]
    row = lax.broadcasted_iota(jnp.int32, (rank, rank), 0)
    column = lax.broadcasted_iota(jnp.int32, (rank, rank), 1)
    diagonal = row == column
    eye = jnp.where(diagonal, 1.0, 0.0)
    matrix = gram + LAMBDA * eye
    along = jnp.where(diagonal, matrix, 0.0)
    down = 1.0 / jnp.sum(along, axis=1, keepdims=True)
    across = 1.0 / jnp.sum(along, axis=0, keepdims=True)
    off = (eye - matrix * across).astype(BF16)
    guess = (eye + (eye - matrix * across)) * down
    guess = guess + dot(guess.astype(BF16), dot(off, off).astype(BF16))
    rest = eye - exact_dot(matrix, guess)
    inverse_ref[...] = guess + exact_dot(guess, rest)
    size = jnp.sum(rest * rest)

    @pl.when(jnp.logical_not(size < 4e-6))
    def _():
        inverse_ref[...] = eliminate(matrix, row, column)

    inverse = inverse_ref[...]
    high, low = split(exact_dot(inverse, gram))
    solve_ref[:, 0:rank] = high
    solve_ref[:, rank : 2 * rank] = low
    high, low = split(inverse)
    solve_ref[:, 2 * rank : 3 * rank] = high
    solve_ref[:, 3 * rank : 4 * rank] = low


def second_pass_kernel(
    scale,
    ids_hbm,
    count_ref,
    vals_hbm,
    cell_hbm,
    gene_hbm,
    sums_ref,
    new_hbm,
    out_ref,
    sem,
    out_sem,
    ids_ref,
    pos_ref,
    vals_ref,
    cell_ref,
    gene_ref,
    solve_ref,
    new_ref,
    turned_ref,
    resid_ref,
    total_ref,
):
    blk = vals_ref.shape[1]
    rank = cell_ref.shape[1]
    gene_blocks = gene_ref.shape[0] // blk
    small, values = start_loads(
        sem, [(ids_hbm, ids_ref), (cell_hbm, cell_ref), (gene_hbm, gene_ref)], (vals_hbm, vals_ref.at[: vals_hbm.shape[0]])
    )
    vals_ref[vals_hbm.shape[0]] = jnp.zeros(vals_ref.shape[1:], BF16)
    small[0].wait()
    fill_positions(ids_ref, count_ref, pos_ref)
    halves = [sums_ref[gene_blocks + i].astype(F32) for i in range(2)]
    gram = jnp.concatenate([half[: rank // 2, :] + half[rank // 2 :, :] for half in halves], axis=0)
    solve_into(solve_ref, total_ref.at[:rank, :], gram)
    for copy in small[1:] + values:
        copy.wait()
    cell_ref[...] = (cell_ref[...].astype(F32) * scale).astype(BF16)
    total_ref[...] = jnp.zeros_like(total_ref)
    stores = []
    low = 0
    for high in SECOND_STAGES:
        for pair in range(low, high):
            rows = pl.ds(2 * pair * blk, 2 * blk)
            sums = jnp.concatenate([sums_ref[2 * pair], sums_ref[2 * pair + 1]], axis=1)
            old = gene_ref[rows, :]
            turned = (
                dot(solve_ref[:, 0:rank], old, NT)
                + dot(solve_ref[:, rank : 2 * rank], old, NT)
                + dot(solve_ref[:, 2 * rank : 4 * rank], jnp.concatenate([sums, sums], axis=0))
            )
            genes = turned.T.astype(BF16)
            turned_ref[:, rows] = turned.astype(BF16)
            new_ref[rows, :] = genes
            residual_pair(vals_ref, pos_ref, resid_ref, dot(cell_ref[...], genes, NT), 2 * pair, gene_blocks, 2 * pair)
        rows = pl.ds(2 * low * blk, 2 * (high - low) * blk)
        total_ref[...] += dot(resid_ref[:, rows], new_ref[rows, :])
        stores.append(pltpu.make_async_copy(new_ref.at[rows], new_hbm.at[rows], out_sem.at[len(stores)]))
        stores[-1].start()
        low = high
    gram = dot(turned_ref[...], new_ref[...])
    owners, out_height, _ = out_ref.shape
    count = total_ref.shape[0] // owners
    lines = out_height - count
    for i in range(owners):
        out_ref[i, :count, :] = total_ref[i * count : (i + 1) * count, :].astype(BF16)
        out_ref[i, count:, :] = gram[i * lines : (i + 1) * lines, :].astype(BF16)
    for store in stores:
        store.wait()


def second_pass(scale, owners, ids, count, values, cells, genes, sums):
    slots, blk, _ = values.shape
    rows, rank = cells.shape
    gene_blocks = genes.shape[0] // blk
    height = (rows + rank) // owners
    return pl.pallas_call(
        functools.partial(second_pass_kernel, scale),
        out_shape=(jax.ShapeDtypeStruct(genes.shape, BF16), jax.ShapeDtypeStruct((owners, height, rank), BF16)),
        in_specs=[HBM, SMEM, HBM, HBM, HBM, VMEM],
        out_specs=(HBM, VMEM),
        scratch_shapes=[
            pltpu.SemaphoreType.DMA((PIECES + 3,)),
            pltpu.SemaphoreType.DMA((len(SECOND_STAGES),)),
            pltpu.SMEM((slots,), jnp.int32),
            pltpu.SMEM((rows // blk * gene_blocks,), jnp.int32),
            pltpu.VMEM((slots + 1, blk, blk), BF16),
            pltpu.VMEM(cells.shape, BF16),
            pltpu.VMEM(genes.shape, BF16),
            pltpu.VMEM((rank, 4 * rank), BF16),
            pltpu.VMEM(genes.shape, BF16),
            pltpu.VMEM((rank, genes.shape[0]), BF16),
            pltpu.VMEM((rows, genes.shape[0]), BF16),
            pltpu.VMEM((rows, rank), F32),
        ],
        compiler_params=PARAMS,
        name="second_pass",
    )(ids, count, values, cells, genes, sums)


def new_cells_kernel(scale, share, cell_ref, sums_ref, out_ref, solve_ref, gram_ref, inverse_ref):
    rank = cell_ref.shape[1]
    senders, height, _ = sums_ref.shape
    half = (height - share) // 2
    for i in range(senders):
        gram = sums_ref[i, share:, :].astype(F32)
        gram_ref[i * half : (i + 1) * half, :] = gram[:half, :] + gram[half:, :]
    solve_into(solve_ref, inverse_ref, gram_ref[...])
    sums = (sums_ref[:, :share, :].reshape(senders * share, rank).astype(F32) * (1.0 / scale)).astype(BF16)
    out_ref[...] = (
        dot(cell_ref[...], solve_ref[:, 0:rank], NT)
        + dot(cell_ref[...], solve_ref[:, rank : 2 * rank], NT)
        + dot(sums, solve_ref[:, 2 * rank : 3 * rank], NT)
        + dot(sums, solve_ref[:, 3 * rank : 4 * rank], NT)
    ).astype(BF16)


def make_new_cells(scale, share, cells, sums):
    rank = cells.shape[1]
    return pl.pallas_call(
        functools.partial(new_cells_kernel, scale, share),
        out_shape=jax.ShapeDtypeStruct(cells.shape, BF16),
        in_specs=[VMEM] * 2,
        out_specs=VMEM,
        scratch_shapes=[
            pltpu.VMEM((rank, 4 * rank), BF16),
            pltpu.VMEM((rank, rank), F32),
            pltpu.VMEM((rank, rank), F32),
        ],
        compiler_params=PARAMS,
        name="new_cells",
    )(cells, sums)


def exchange(parts, axis, groups=None):
    return lax.all_to_all(parts, axis, 0, 0, tiled=True, axis_index_groups=groups)


def across_cells(blocks):
    owners = blocks.shape[0]
    outer = owners // INNER
    inner_groups = [[o * INNER + i for i in range(INNER)] for o in range(outer)]
    outer_groups = [[o * INNER + i for o in range(outer)] for i in range(INNER)]
    parts = exchange(blocks, "cell", inner_groups).reshape((INNER, outer) + blocks.shape[1:])
    parts = exchange(add_blocks(0, 1, owners - 2, parts)[0], "cell", outer_groups)
    parts = exchange(add_blocks(1, outer, owners - 2, parts[:, None])[:, 0], "cell", outer_groups)
    return exchange(repeat(INNER, parts).reshape(blocks.shape), "cell", inner_groups)


def body(block_values, block_ids, block_count, cell_factor, gene_factor):
    values = block_values[0, 0]
    ids = block_ids[0, 0]
    count = block_count[0]
    rows = cell_factor.shape[0]
    n_cell, n_gene = lax.axis_size("cell"), lax.axis_size("gene")
    scale = (rows * n_cell) ** (-0.5)
    cell_share = rows // n_gene

    sums = across_cells(first_pass(scale, ids, count, values, cell_factor, gene_factor))
    new_genes, cell_terms = second_pass(scale, n_gene, ids, count, values, cell_factor, gene_factor, sums)
    cell_sums = exchange(add_cells(cell_share, exchange(cell_terms, "gene")), "gene")
    new_cells = make_new_cells(scale, cell_share, cell_factor, cell_sums)
    return new_cells, new_genes


def solution(mesh):
    return jax.shard_map(
        body,
        mesh=mesh,
        in_specs=(
            P("cell", "gene", None, None, None),
            P("cell", "gene", None),
            P("cell", "gene"),
            P("cell", None),
            P("gene", None),
        ),
        out_specs=(P("cell", None), P("gene", None)),
        check_vma=False,
    )
```

```python
import functools

import jax
import jax.numpy as jnp
from jax import lax
from jax.experimental import pallas as pl
from jax.experimental.pallas import tpu as pltpu
from jax.sharding import PartitionSpec as P

LAMBDA = 0.5
F32 = jnp.float32
BF16 = jnp.bfloat16
NN = (((1,), (0,)), ((), ()))
NT = (((1,), (1,)), ((), ()))
PARAMS = pltpu.CompilerParams(vmem_limit_bytes=48 * 1024 * 1024)
SMEM = pl.BlockSpec(memory_space=pltpu.SMEM)
VMEM = pl.BlockSpec(memory_space=pltpu.VMEM)
HBM = pl.BlockSpec(memory_space=pltpu.HBM)
FIRST_STAGES = (5, 10, 15)
AHEAD = 8
PIECES = 1
INNER = 4


def dot(a, b, dims=NN):
    return lax.dot_general(a, b, dims, preferred_element_type=F32)


def exact_dot(a, b):
    return lax.dot_general(a, b, NN, precision=lax.Precision.HIGHEST, preferred_element_type=F32)


def split(value):
    high = value.astype(BF16)
    return high, (value - high.astype(F32)).astype(BF16)


def two_terms(value):
    high = value.astype(BF16).astype(F32)
    return jnp.concatenate([high, value - high], axis=0).astype(BF16)


def start_loads(sem, small, large):
    copies = [pltpu.make_async_copy(source, target, sem.at[i]) for i, (source, target) in enumerate(small)]
    source, target = large
    step = source.shape[0] // PIECES
    for i in range(PIECES):
        part = pl.ds(i * step, step)
        copies.append(pltpu.make_async_copy(source.at[part], target.at[part], sem.at[len(small) + i]))
    for copy in copies:
        copy.start()
    return copies[: len(small)], copies[len(small) :]


def fill_positions(ids_ref, count_ref, pos_ref):
    slots = ids_ref.shape[0]
    for i in range(pos_ref.shape[0]):
        pos_ref[i] = slots
    count = count_ref[0]
    for k in range(slots):
        pos_ref[ids_ref[k]] = jnp.where(k < count, k, slots)


def residual_pair(vals_ref, pos_ref, resid_ref, fit, first, gene_blocks, at):
    blk = vals_ref.shape[1]
    for c in range(fit.shape[0] // blk):
        for h in range(2):
            value = vals_ref[pos_ref[c * gene_blocks + first + h]].astype(F32)
            part = value - fit[c * blk : (c + 1) * blk, h * blk : (h + 1) * blk]
            to = pl.ds((at + h) * blk, blk)
            resid_ref[pl.ds(c * blk, blk), to] = jnp.where(value != 0.0, part, 0.0).astype(BF16)


def first_pass_kernel(
    scale,
    gene_blocks,
    ids_hbm,
    count_ref,
    vals_hbm,
    cell_hbm,
    gene_hbm,
    out_hbm,
    sem,
    out_sem,
    ids_ref,
    pos_ref,
    vals_ref,
    cell_ref,
    gene_ref,
    turned_ref,
    fit_ref,
    resid_ref,
    out_ref,
):
    blk = vals_ref.shape[1]
    rank = cell_ref.shape[1]
    small, values = start_loads(
        sem, [(ids_hbm, ids_ref), (cell_hbm, cell_ref), (gene_hbm, gene_ref)], (vals_hbm, vals_ref.at[: vals_hbm.shape[0]])
    )
    vals_ref[vals_hbm.shape[0]] = jnp.zeros(vals_ref.shape[1:], BF16)
    small[1].wait()
    scaled = cell_ref[...].astype(F32) * scale
    turned_ref[...] = scaled.T.astype(BF16)
    cell_ref[...] = scaled.astype(BF16)
    gram = dot(turned_ref[...], cell_ref[...])
    out_ref[gene_blocks] = two_terms(gram[: rank // 2, :])
    out_ref[gene_blocks + 1] = two_terms(gram[rank // 2 :, :])
    small[2].wait()

    def fit_of(pair):
        return dot(cell_ref[...], gene_ref[2 * pair * blk : 2 * (pair + 1) * blk, :], NT)

    ahead = fit_ref.shape[0]
    for pair in range(ahead):
        fit_ref[pair] = fit_of(pair)
    small[0].wait()
    fill_positions(ids_ref, count_ref, pos_ref)
    for copy in values:
        copy.wait()

    stores = []
    low = 0
    for high in FIRST_STAGES:
        for pair in range(low, high):
            fit = fit_ref[pair] if pair < ahead else fit_of(pair)
            residual_pair(vals_ref, pos_ref, resid_ref, fit, 2 * pair, gene_blocks, 2 * pair)
        terms = dot(turned_ref[...], resid_ref[:, 2 * low * blk : 2 * high * blk]).astype(BF16)
        for u in range(2 * (high - low)):
            out_ref[2 * low + u] = terms[:, u * blk : (u + 1) * blk]
        to = pl.ds(2 * low, 2 * (high - low) + (2 if high == FIRST_STAGES[-1] else 0))
        stores.append(pltpu.make_async_copy(out_ref.at[to], out_hbm.at[to], out_sem.at[len(stores)]))
        stores[-1].start()
        low = high
    for store in stores:
        store.wait()


def first_pass(scale, ids, count, values, cells, genes):
    slots, blk, _ = values.shape
    rows, rank = cells.shape
    gene_blocks = genes.shape[0] // blk
    return pl.pallas_call(
        functools.partial(first_pass_kernel, scale, gene_blocks),
        out_shape=jax.ShapeDtypeStruct((gene_blocks + 2, rank, blk), BF16),
        in_specs=[HBM, SMEM, HBM, HBM, HBM],
        out_specs=HBM,
        scratch_shapes=[
            pltpu.SemaphoreType.DMA((PIECES + 3,)),
            pltpu.SemaphoreType.DMA((len(FIRST_STAGES),)),
            pltpu.SMEM((slots,), jnp.int32),
            pltpu.SMEM((rows // blk * gene_blocks,), jnp.int32),
            pltpu.VMEM((slots + 1, blk, blk), BF16),
            pltpu.VMEM(cells.shape, BF16),
            pltpu.VMEM(genes.shape, BF16),
            pltpu.VMEM((rank, rows), BF16),
            pltpu.VMEM((AHEAD, rows, 2 * blk), F32),
            pltpu.VMEM((rows, genes.shape[0]), BF16),
            pltpu.VMEM((gene_blocks + 2, rank, blk), BF16),
        ],
        compiler_params=pltpu.CompilerParams(vmem_limit_bytes=63 * 1024 * 1024),
        name="first_pass",
    )(ids, count, values, cells, genes)


def total_of(parts_ref, slot, rows):
    total = parts_ref[0, slot, rows, :].astype(F32)
    for i in range(1, parts_ref.shape[0]):
        total = total + parts_ref[i, slot, rows, :].astype(F32)
    return total


def add_blocks_kernel(stage, gram_from, parts_ref, out_ref):
    parts, slots, height, _ = parts_ref.shape
    place = lax.axis_index("cell")
    outer = lax.axis_size("cell") // INNER
    first = (place % INNER) * outer + (place // INNER if stage else 0)
    step = height // 4
    for slot in range(slots):
        may_be_gram = stage or slot >= gram_from % outer
        if may_be_gram:
            whole = total_of(parts_ref, slot, pl.ds(0, height))
            is_gram = first + slot >= gram_from
            gram = two_terms(whole[: height // 2, :] + whole[height // 2 :, :]).astype(F32)
            whole = jnp.where(is_gram, gram, whole).astype(BF16)
            for i in range(out_ref.shape[0]):
                out_ref[i, slot] = whole
        else:
            for low in range(0, height, step):
                rows = pl.ds(low, step)
                out_ref[0, slot, rows, :] = total_of(parts_ref, slot, rows).astype(BF16)


def add_blocks(stage, copies, gram_from, parts):
    return pl.pallas_call(
        functools.partial(add_blocks_kernel, stage, gram_from),
        out_shape=jax.ShapeDtypeStruct((copies,) + parts.shape[1:], BF16),
        in_specs=[VMEM],
        out_specs=VMEM,
        compiler_params=PARAMS,
        name="add_blocks",
    )(parts)


def repeat_kernel(part_ref, out_ref):
    for slot in range(part_ref.shape[0]):
        block = part_ref[slot]
        for i in range(out_ref.shape[0]):
            out_ref[i, slot] = block


def repeat(copies, part):
    return pl.pallas_call(
        repeat_kernel,
        out_shape=jax.ShapeDtypeStruct((copies,) + part.shape, BF16),
        in_specs=[VMEM],
        out_specs=VMEM,
        compiler_params=PARAMS,
        name="repeat",
    )(part)


def add_cells_kernel(parts_ref, out_ref):
    value = parts_ref[0].astype(F32)
    for i in range(1, parts_ref.shape[0]):
        value = value + parts_ref[i].astype(F32)
    total = value.astype(BF16)
    for i in range(out_ref.shape[0]):
        out_ref[i] = total


def add_cells(parts):
    return pl.pallas_call(
        add_cells_kernel,
        out_shape=jax.ShapeDtypeStruct(parts.shape, BF16),
        in_specs=[VMEM],
        out_specs=VMEM,
        compiler_params=PARAMS,
        name="add_cells",
    )(parts)


def eliminate(work, row, column):
    for k in range(work.shape[0]):
        at_row = row[:, 0:1] == k
        at_column = column[0:1, :] == k
        line = work[k : k + 1, :]
        pivot = 1.0 / work[k : k + 1, k : k + 1]
        side = work[:, k : k + 1] - jnp.where(at_row, 1.0, 0.0)
        line = jnp.where(at_column, 1.0, line) * pivot
        kept = jnp.where(at_column, jnp.where(at_row, 1.0, 0.0), work)
        work = kept - side * line
    return work


def solve_into(solve_ref, inverse_ref, gram):
    rank = gram.shape[0]
    row = lax.broadcasted_iota(jnp.int32, (rank, rank), 0)
    column = lax.broadcasted_iota(jnp.int32, (rank, rank), 1)
    diagonal = row == column
    eye = jnp.where(diagonal, 1.0, 0.0)
    matrix = gram + LAMBDA * eye
    along = jnp.where(diagonal, matrix, 0.0)
    down = 1.0 / jnp.sum(along, axis=1, keepdims=True)
    across = 1.0 / jnp.sum(along, axis=0, keepdims=True)
    off = (eye - matrix * across).astype(BF16)
    guess = (eye + (eye - matrix * across)) * down
    guess = guess + dot(guess.astype(BF16), dot(off, off).astype(BF16))
    rest = eye - exact_dot(matrix, guess)
    inverse_ref[...] = guess + exact_dot(guess, rest)
    size = jnp.sum(rest * rest)

    @pl.when(jnp.logical_not(size < 4e-6))
    def _():
        inverse_ref[...] = eliminate(matrix, row, column)

    inverse = inverse_ref[...]
    high, low = split(exact_dot(inverse, gram))
    solve_ref[:, 0:rank] = high
    solve_ref[:, rank : 2 * rank] = low
    high, low = split(inverse)
    solve_ref[:, 2 * rank : 3 * rank] = high
    solve_ref[:, 3 * rank : 4 * rank] = low


def second_pass_kernel(
    scale,
    ids_hbm,
    count_ref,
    vals_hbm,
    cell_hbm,
    gene_hbm,
    sums_ref,
    new_hbm,
    out_ref,
    sem,
    out_sem,
    ids_ref,
    pos_ref,
    vals_ref,
    cell_ref,
    gene_ref,
    solve_ref,
    new_ref,
    turned_ref,
    resid_ref,
    total_ref,
):
    blk = vals_ref.shape[1]
    rank = cell_ref.shape[1]
    gene_blocks = gene_ref.shape[0] // blk
    small, values = start_loads(
        sem, [(ids_hbm, ids_ref), (cell_hbm, cell_ref), (gene_hbm, gene_ref)], (vals_hbm, vals_ref.at[: vals_hbm.shape[0]])
    )
    vals_ref[vals_hbm.shape[0]] = jnp.zeros(vals_ref.shape[1:], BF16)
    small[0].wait()
    fill_positions(ids_ref, count_ref, pos_ref)
    halves = [sums_ref[gene_blocks + i].astype(F32) for i in range(2)]
    gram = jnp.concatenate([half[: rank // 2, :] + half[rank // 2 :, :] for half in halves], axis=0)
    solve_into(solve_ref, total_ref.at[:rank, :], gram)
    for copy in small[1:]:
        copy.wait()
    cell_ref[...] = (cell_ref[...].astype(F32) * scale).astype(BF16)
    pairs = gene_blocks // 2
    for pair in range(pairs):
        rows = pl.ds(2 * pair * blk, 2 * blk)
        sums = jnp.concatenate([sums_ref[2 * pair], sums_ref[2 * pair + 1]], axis=1)
        old = gene_ref[rows, :]
        turned = (
            dot(solve_ref[:, 0:rank], old, NT)
            + dot(solve_ref[:, rank : 2 * rank], old, NT)
            + dot(solve_ref[:, 2 * rank : 4 * rank], jnp.concatenate([sums, sums], axis=0))
        )
        new_ref[rows, :] = turned.T.astype(BF16)
        turned_ref[:, rows] = turned.astype(BF16)
    store = pltpu.make_async_copy(new_ref, new_hbm, out_sem)
    store.start()
    gram = dot(turned_ref[...], new_ref[...])
    for copy in values:
        copy.wait()
    for pair in range(pairs):
        genes = new_ref[2 * pair * blk : 2 * (pair + 1) * blk, :]
        residual_pair(vals_ref, pos_ref, resid_ref, dot(cell_ref[...], genes, NT), 2 * pair, gene_blocks, 2 * pair)
    total_ref[...] = dot(resid_ref[...], new_ref[...])
    owners, out_height, _ = out_ref.shape
    count = total_ref.shape[0] // owners
    lines = out_height - count
    for i in range(owners):
        out_ref[i, :count, :] = total_ref[i * count : (i + 1) * count, :].astype(BF16)
        out_ref[i, count:, :] = gram[i * lines : (i + 1) * lines, :].astype(BF16)
    store.wait()


def second_pass(scale, owners, ids, count, values, cells, genes, sums):
    slots, blk, _ = values.shape
    rows, rank = cells.shape
    gene_blocks = genes.shape[0] // blk
    height = (rows + rank) // owners
    return pl.pallas_call(
        functools.partial(second_pass_kernel, scale),
        out_shape=(jax.ShapeDtypeStruct(genes.shape, BF16), jax.ShapeDtypeStruct((owners, height, rank), BF16)),
        in_specs=[HBM, SMEM, HBM, HBM, HBM, VMEM],
        out_specs=(HBM, VMEM),
        scratch_shapes=[
            pltpu.SemaphoreType.DMA((PIECES + 3,)),
            pltpu.SemaphoreType.DMA,
            pltpu.SMEM((slots,), jnp.int32),
            pltpu.SMEM((rows // blk * gene_blocks,), jnp.int32),
            pltpu.VMEM((slots + 1, blk, blk), BF16),
            pltpu.VMEM(cells.shape, BF16),
            pltpu.VMEM(genes.shape, BF16),
            pltpu.VMEM((rank, 4 * rank), BF16),
            pltpu.VMEM(genes.shape, BF16),
            pltpu.VMEM((rank, genes.shape[0]), BF16),
            pltpu.VMEM((rows, genes.shape[0]), BF16),
            pltpu.VMEM((rows, rank), F32),
        ],
        compiler_params=PARAMS,
        name="second_pass",
    )(ids, count, values, cells, genes, sums)


def new_cells_kernel(scale, share, cell_ref, sums_ref, out_ref, solve_ref, gram_ref, inverse_ref):
    rank = cell_ref.shape[1]
    senders, height, _ = sums_ref.shape
    lines = height - share
    for i in range(senders):
        gram_ref[i * lines : (i + 1) * lines, :] = sums_ref[i, share:, :].astype(F32)
    solve_into(solve_ref, inverse_ref, gram_ref[...])
    sums = (sums_ref[:, :share, :].reshape(senders * share, rank).astype(F32) * (1.0 / scale)).astype(BF16)
    out_ref[...] = (
        dot(cell_ref[...], solve_ref[:, 0:rank], NT)
        + dot(cell_ref[...], solve_ref[:, rank : 2 * rank], NT)
        + dot(sums, solve_ref[:, 2 * rank : 3 * rank], NT)
        + dot(sums, solve_ref[:, 3 * rank : 4 * rank], NT)
    ).astype(BF16)


def make_new_cells(scale, share, cells, sums):
    rank = cells.shape[1]
    return pl.pallas_call(
        functools.partial(new_cells_kernel, scale, share),
        out_shape=jax.ShapeDtypeStruct(cells.shape, BF16),
        in_specs=[VMEM] * 2,
        out_specs=VMEM,
        scratch_shapes=[
            pltpu.VMEM((rank, 4 * rank), BF16),
            pltpu.VMEM((rank, rank), F32),
            pltpu.VMEM((rank, rank), F32),
        ],
        compiler_params=PARAMS,
        name="new_cells",
    )(cells, sums)


def exchange(parts, axis, groups=None):
    return lax.all_to_all(parts, axis, 0, 0, tiled=True, axis_index_groups=groups)


def across_cells(blocks):
    owners = blocks.shape[0]
    outer = owners // INNER
    inner_groups = [[o * INNER + i for i in range(INNER)] for o in range(outer)]
    outer_groups = [[o * INNER + i for o in range(outer)] for i in range(INNER)]
    parts = exchange(blocks, "cell", inner_groups).reshape((INNER, outer) + blocks.shape[1:])
    parts = exchange(add_blocks(0, 1, owners - 2, parts)[0], "cell", outer_groups)
    parts = exchange(add_blocks(1, outer, owners - 2, parts[:, None])[:, 0], "cell", outer_groups)
    return exchange(repeat(INNER, parts).reshape(blocks.shape), "cell", inner_groups)


def body(block_values, block_ids, block_count, cell_factor, gene_factor):
    values = block_values[0, 0]
    ids = block_ids[0, 0]
    count = block_count[0]
    rows = cell_factor.shape[0]
    n_cell, n_gene = lax.axis_size("cell"), lax.axis_size("gene")
    scale = (rows * n_cell) ** (-0.5)
    cell_share = rows // n_gene

    sums = across_cells(first_pass(scale, ids, count, values, cell_factor, gene_factor))
    new_genes, cell_terms = second_pass(scale, n_gene, ids, count, values, cell_factor, gene_factor, sums)
    cell_sums = exchange(add_cells(exchange(cell_terms, "gene")), "gene")
    new_cells = make_new_cells(scale, cell_share, cell_factor, cell_sums)
    return new_cells, new_genes


def solution(mesh):
    return jax.shard_map(
        body,
        mesh=mesh,
        in_specs=(
            P("cell", "gene", None, None, None),
            P("cell", "gene", None),
            P("cell", "gene"),
            P("cell", None),
            P("gene", None),
        ),
        out_specs=(P("cell", None), P("gene", None)),
        check_vma=False,
    )
```

```python
import functools

import jax
import jax.numpy as jnp
from jax import lax
from jax.experimental import pallas as pl
from jax.experimental.pallas import tpu as pltpu
from jax.sharding import PartitionSpec as P

LAMBDA = 0.5
F32 = jnp.float32
BF16 = jnp.bfloat16
NN = (((1,), (0,)), ((), ()))
NT = (((1,), (1,)), ((), ()))
PARAMS = pltpu.CompilerParams(vmem_limit_bytes=48 * 1024 * 1024)
SMEM = pl.BlockSpec(memory_space=pltpu.SMEM)
VMEM = pl.BlockSpec(memory_space=pltpu.VMEM)
HBM = pl.BlockSpec(memory_space=pltpu.HBM)
FIRST_STAGES = (5, 10, 15)
AHEAD = 8
PIECES = 1
INNER = 8


def dot(a, b, dims=NN):
    return lax.dot_general(a, b, dims, preferred_element_type=F32)


def exact_dot(a, b):
    return lax.dot_general(a, b, NN, precision=lax.Precision.HIGHEST, preferred_element_type=F32)


def split(value):
    high = value.astype(BF16)
    return high, (value - high.astype(F32)).astype(BF16)


def two_terms(value):
    high = value.astype(BF16).astype(F32)
    return jnp.concatenate([high, value - high], axis=0).astype(BF16)


def start_loads(sem, small, large):
    copies = [pltpu.make_async_copy(source, target, sem.at[i]) for i, (source, target) in enumerate(small)]
    source, target = large
    step = source.shape[0] // PIECES
    for i in range(PIECES):
        part = pl.ds(i * step, step)
        copies.append(pltpu.make_async_copy(source.at[part], target.at[part], sem.at[len(small) + i]))
    for copy in copies:
        copy.start()
    return copies[: len(small)], copies[len(small) :]


def fill_positions(ids_ref, count_ref, pos_ref):
    slots = ids_ref.shape[0]
    for i in range(pos_ref.shape[0]):
        pos_ref[i] = slots
    count = count_ref[0]
    for k in range(slots):
        pos_ref[ids_ref[k]] = jnp.where(k < count, k, slots)


def residual_pair(vals_ref, pos_ref, resid_ref, fit, first, gene_blocks, at):
    blk = vals_ref.shape[1]
    for c in range(fit.shape[0] // blk):
        for h in range(2):
            value = vals_ref[pos_ref[c * gene_blocks + first + h]].astype(F32)
            part = value - fit[c * blk : (c + 1) * blk, h * blk : (h + 1) * blk]
            to = pl.ds((at + h) * blk, blk)
            resid_ref[pl.ds(c * blk, blk), to] = jnp.where(value != 0.0, part, 0.0).astype(BF16)


def first_pass_kernel(
    scale,
    gene_blocks,
    ids_hbm,
    count_ref,
    vals_hbm,
    cell_hbm,
    gene_hbm,
    out_hbm,
    sem,
    out_sem,
    ids_ref,
    pos_ref,
    vals_ref,
    cell_ref,
    gene_ref,
    turned_ref,
    fit_ref,
    resid_ref,
    out_ref,
):
    blk = vals_ref.shape[1]
    rank = cell_ref.shape[1]
    small, values = start_loads(
        sem, [(ids_hbm, ids_ref), (cell_hbm, cell_ref), (gene_hbm, gene_ref)], (vals_hbm, vals_ref.at[: vals_hbm.shape[0]])
    )
    vals_ref[vals_hbm.shape[0]] = jnp.zeros(vals_ref.shape[1:], BF16)
    small[1].wait()
    scaled = cell_ref[...].astype(F32) * scale
    turned_ref[...] = scaled.T.astype(BF16)
    cell_ref[...] = scaled.astype(BF16)
    gram = dot(turned_ref[...], cell_ref[...])
    out_ref[gene_blocks] = two_terms(gram[: rank // 2, :])
    out_ref[gene_blocks + 1] = two_terms(gram[rank // 2 :, :])
    small[2].wait()

    def fit_of(pair):
        return dot(cell_ref[...], gene_ref[2 * pair * blk : 2 * (pair + 1) * blk, :], NT)

    ahead = fit_ref.shape[0]
    for pair in range(ahead):
        fit_ref[pair] = fit_of(pair)
    small[0].wait()
    fill_positions(ids_ref, count_ref, pos_ref)
    for copy in values:
        copy.wait()

    stores = []
    low = 0
    for high in FIRST_STAGES:
        for pair in range(low, high):
            fit = fit_ref[pair] if pair < ahead else fit_of(pair)
            residual_pair(vals_ref, pos_ref, resid_ref, fit, 2 * pair, gene_blocks, 2 * pair)
        terms = dot(turned_ref[...], resid_ref[:, 2 * low * blk : 2 * high * blk]).astype(BF16)
        for u in range(2 * (high - low)):
            out_ref[2 * low + u] = terms[:, u * blk : (u + 1) * blk]
        to = pl.ds(2 * low, 2 * (high - low) + (2 if high == FIRST_STAGES[-1] else 0))
        stores.append(pltpu.make_async_copy(out_ref.at[to], out_hbm.at[to], out_sem.at[len(stores)]))
        stores[-1].start()
        low = high
    for store in stores:
        store.wait()


def first_pass(scale, ids, count, values, cells, genes):
    slots, blk, _ = values.shape
    rows, rank = cells.shape
    gene_blocks = genes.shape[0] // blk
    return pl.pallas_call(
        functools.partial(first_pass_kernel, scale, gene_blocks),
        out_shape=jax.ShapeDtypeStruct((gene_blocks + 2, rank, blk), BF16),
        in_specs=[HBM, SMEM, HBM, HBM, HBM],
        out_specs=HBM,
        scratch_shapes=[
            pltpu.SemaphoreType.DMA((PIECES + 3,)),
            pltpu.SemaphoreType.DMA((len(FIRST_STAGES),)),
            pltpu.SMEM((slots,), jnp.int32),
            pltpu.SMEM((rows // blk * gene_blocks,), jnp.int32),
            pltpu.VMEM((slots + 1, blk, blk), BF16),
            pltpu.VMEM(cells.shape, BF16),
            pltpu.VMEM(genes.shape, BF16),
            pltpu.VMEM((rank, rows), BF16),
            pltpu.VMEM((AHEAD, rows, 2 * blk), F32),
            pltpu.VMEM((rows, genes.shape[0]), BF16),
            pltpu.VMEM((gene_blocks + 2, rank, blk), BF16),
        ],
        compiler_params=pltpu.CompilerParams(vmem_limit_bytes=63 * 1024 * 1024),
        name="first_pass",
    )(ids, count, values, cells, genes)


def total_of(parts_ref, slot, rows):
    total = parts_ref[0, slot, rows, :].astype(F32)
    for i in range(1, parts_ref.shape[0]):
        total = total + parts_ref[i, slot, rows, :].astype(F32)
    return total


def add_blocks_kernel(stage, gram_from, parts_ref, out_ref):
    parts, slots, height, _ = parts_ref.shape
    place = lax.axis_index("cell")
    outer = lax.axis_size("cell") // INNER
    first = (place % INNER) * outer + (place // INNER if stage else 0)
    step = height // 4
    for slot in range(slots):
        may_be_gram = stage or slot >= gram_from % outer
        if may_be_gram:
            whole = total_of(parts_ref, slot, pl.ds(0, height))
            is_gram = first + slot >= gram_from
            gram = two_terms(whole[: height // 2, :] + whole[height // 2 :, :]).astype(F32)
            whole = jnp.where(is_gram, gram, whole).astype(BF16)
            for i in range(out_ref.shape[0]):
                out_ref[i, slot] = whole
        else:
            for low in range(0, height, step):
                rows = pl.ds(low, step)
                out_ref[0, slot, rows, :] = total_of(parts_ref, slot, rows).astype(BF16)


def add_blocks(stage, copies, gram_from, parts):
    return pl.pallas_call(
        functools.partial(add_blocks_kernel, stage, gram_from),
        out_shape=jax.ShapeDtypeStruct((copies,) + parts.shape[1:], BF16),
        in_specs=[VMEM],
        out_specs=VMEM,
        compiler_params=PARAMS,
        name="add_blocks",
    )(parts)


def repeat_kernel(part_ref, out_ref):
    for slot in range(part_ref.shape[0]):
        block = part_ref[slot]
        for i in range(out_ref.shape[0]):
            out_ref[i, slot] = block


def repeat(copies, part):
    return pl.pallas_call(
        repeat_kernel,
        out_shape=jax.ShapeDtypeStruct((copies,) + part.shape, BF16),
        in_specs=[VMEM],
        out_specs=VMEM,
        compiler_params=PARAMS,
        name="repeat",
    )(part)


def add_cells_kernel(parts_ref, out_ref):
    value = parts_ref[0].astype(F32)
    for i in range(1, parts_ref.shape[0]):
        value = value + parts_ref[i].astype(F32)
    total = value.astype(BF16)
    for i in range(out_ref.shape[0]):
        out_ref[i] = total


def add_cells(parts):
    return pl.pallas_call(
        add_cells_kernel,
        out_shape=jax.ShapeDtypeStruct(parts.shape, BF16),
        in_specs=[VMEM],
        out_specs=VMEM,
        compiler_params=PARAMS,
        name="add_cells",
    )(parts)


def eliminate(work, row, column):
    for k in range(work.shape[0]):
        at_row = row[:, 0:1] == k
        at_column = column[0:1, :] == k
        line = work[k : k + 1, :]
        pivot = 1.0 / work[k : k + 1, k : k + 1]
        side = work[:, k : k + 1] - jnp.where(at_row, 1.0, 0.0)
        line = jnp.where(at_column, 1.0, line) * pivot
        kept = jnp.where(at_column, jnp.where(at_row, 1.0, 0.0), work)
        work = kept - side * line
    return work


def solve_into(solve_ref, inverse_ref, gram):
    rank = gram.shape[0]
    row = lax.broadcasted_iota(jnp.int32, (rank, rank), 0)
    column = lax.broadcasted_iota(jnp.int32, (rank, rank), 1)
    diagonal = row == column
    eye = jnp.where(diagonal, 1.0, 0.0)
    matrix = gram + LAMBDA * eye
    along = jnp.where(diagonal, matrix, 0.0)
    down = 1.0 / jnp.sum(along, axis=1, keepdims=True)
    across = 1.0 / jnp.sum(along, axis=0, keepdims=True)
    off = (eye - matrix * across).astype(BF16)
    guess = (eye + (eye - matrix * across)) * down
    guess = guess + dot(guess.astype(BF16), dot(off, off).astype(BF16))
    rest = eye - exact_dot(matrix, guess)
    inverse_ref[...] = guess + exact_dot(guess, rest)
    size = jnp.sum(rest * rest)

    @pl.when(jnp.logical_not(size < 4e-6))
    def _():
        inverse_ref[...] = eliminate(matrix, row, column)

    inverse = inverse_ref[...]
    high, low = split(exact_dot(inverse, gram))
    solve_ref[:, 0:rank] = high
    solve_ref[:, rank : 2 * rank] = low
    high, low = split(inverse)
    solve_ref[:, 2 * rank : 3 * rank] = high
    solve_ref[:, 3 * rank : 4 * rank] = low


def second_pass_kernel(
    scale,
    ids_hbm,
    count_ref,
    vals_hbm,
    cell_hbm,
    gene_hbm,
    sums_ref,
    new_hbm,
    out_ref,
    sem,
    out_sem,
    ids_ref,
    pos_ref,
    vals_ref,
    cell_ref,
    gene_ref,
    solve_ref,
    new_ref,
    turned_ref,
    resid_ref,
    total_ref,
):
    blk = vals_ref.shape[1]
    rank = cell_ref.shape[1]
    gene_blocks = gene_ref.shape[0] // blk
    small, values = start_loads(
        sem, [(ids_hbm, ids_ref), (cell_hbm, cell_ref), (gene_hbm, gene_ref)], (vals_hbm, vals_ref.at[: vals_hbm.shape[0]])
    )
    vals_ref[vals_hbm.shape[0]] = jnp.zeros(vals_ref.shape[1:], BF16)
    small[0].wait()
    fill_positions(ids_ref, count_ref, pos_ref)
    halves = [sums_ref[gene_blocks + i].astype(F32) for i in range(2)]
    gram = jnp.concatenate([half[: rank // 2, :] + half[rank // 2 :, :] for half in halves], axis=0)
    solve_into(solve_ref, total_ref.at[:rank, :], gram)
    for copy in small[1:]:
        copy.wait()
    cell_ref[...] = (cell_ref[...].astype(F32) * scale).astype(BF16)
    pairs = gene_blocks // 2
    for pair in range(pairs):
        rows = pl.ds(2 * pair * blk, 2 * blk)
        sums = jnp.concatenate([sums_ref[2 * pair], sums_ref[2 * pair + 1]], axis=1)
        old = gene_ref[rows, :]
        turned = (
            dot(solve_ref[:, 0:rank], old, NT)
            + dot(solve_ref[:, rank : 2 * rank], old, NT)
            + dot(solve_ref[:, 2 * rank : 4 * rank], jnp.concatenate([sums, sums], axis=0))
        )
        new_ref[rows, :] = turned.T.astype(BF16)
        turned_ref[:, rows] = turned.astype(BF16)
    store = pltpu.make_async_copy(new_ref, new_hbm, out_sem)
    store.start()
    gram = dot(turned_ref[...], new_ref[...])
    for copy in values:
        copy.wait()
    for pair in range(pairs):
        genes = new_ref[2 * pair * blk : 2 * (pair + 1) * blk, :]
        residual_pair(vals_ref, pos_ref, resid_ref, dot(cell_ref[...], genes, NT), 2 * pair, gene_blocks, 2 * pair)
    total_ref[...] = dot(resid_ref[...], new_ref[...])
    owners, out_height, _ = out_ref.shape
    count = total_ref.shape[0] // owners
    lines = out_height - count
    for i in range(owners):
        out_ref[i, :count, :] = total_ref[i * count : (i + 1) * count, :].astype(BF16)
        out_ref[i, count:, :] = gram[i * lines : (i + 1) * lines, :].astype(BF16)
    store.wait()


def second_pass(scale, owners, ids, count, values, cells, genes, sums):
    slots, blk, _ = values.shape
    rows, rank = cells.shape
    gene_blocks = genes.shape[0] // blk
    height = (rows + rank) // owners
    return pl.pallas_call(
        functools.partial(second_pass_kernel, scale),
        out_shape=(jax.ShapeDtypeStruct(genes.shape, BF16), jax.ShapeDtypeStruct((owners, height, rank), BF16)),
        in_specs=[HBM, SMEM, HBM, HBM, HBM, VMEM],
        out_specs=(HBM, VMEM),
        scratch_shapes=[
            pltpu.SemaphoreType.DMA((PIECES + 3,)),
            pltpu.SemaphoreType.DMA,
            pltpu.SMEM((slots,), jnp.int32),
            pltpu.SMEM((rows // blk * gene_blocks,), jnp.int32),
            pltpu.VMEM((slots + 1, blk, blk), BF16),
            pltpu.VMEM(cells.shape, BF16),
            pltpu.VMEM(genes.shape, BF16),
            pltpu.VMEM((rank, 4 * rank), BF16),
            pltpu.VMEM(genes.shape, BF16),
            pltpu.VMEM((rank, genes.shape[0]), BF16),
            pltpu.VMEM((rows, genes.shape[0]), BF16),
            pltpu.VMEM((rows, rank), F32),
        ],
        compiler_params=PARAMS,
        name="second_pass",
    )(ids, count, values, cells, genes, sums)


def new_cells_kernel(scale, share, cell_ref, sums_ref, out_ref, solve_ref, gram_ref, inverse_ref):
    rank = cell_ref.shape[1]
    senders, height, _ = sums_ref.shape
    lines = height - share
    for i in range(senders):
        gram_ref[i * lines : (i + 1) * lines, :] = sums_ref[i, share:, :].astype(F32)
    solve_into(solve_ref, inverse_ref, gram_ref[...])
    sums = (sums_ref[:, :share, :].reshape(senders * share, rank).astype(F32) * (1.0 / scale)).astype(BF16)
    out_ref[...] = (
        dot(cell_ref[...], solve_ref[:, 0:rank], NT)
        + dot(cell_ref[...], solve_ref[:, rank : 2 * rank], NT)
        + dot(sums, solve_ref[:, 2 * rank : 3 * rank], NT)
        + dot(sums, solve_ref[:, 3 * rank : 4 * rank], NT)
    ).astype(BF16)


def make_new_cells(scale, share, cells, sums):
    rank = cells.shape[1]
    return pl.pallas_call(
        functools.partial(new_cells_kernel, scale, share),
        out_shape=jax.ShapeDtypeStruct(cells.shape, BF16),
        in_specs=[VMEM] * 2,
        out_specs=VMEM,
        scratch_shapes=[
            pltpu.VMEM((rank, 4 * rank), BF16),
            pltpu.VMEM((rank, rank), F32),
            pltpu.VMEM((rank, rank), F32),
        ],
        compiler_params=PARAMS,
        name="new_cells",
    )(cells, sums)


def exchange(parts, axis, groups=None):
    return lax.all_to_all(parts, axis, 0, 0, tiled=True, axis_index_groups=groups)


def across_cells(blocks):
    owners = blocks.shape[0]
    outer = owners // INNER
    inner_groups = [[o * INNER + i for i in range(INNER)] for o in range(outer)]
    outer_groups = [[o * INNER + i for o in range(outer)] for i in range(INNER)]
    parts = exchange(blocks, "cell", inner_groups).reshape((INNER, outer) + blocks.shape[1:])
    parts = exchange(add_blocks(0, 1, owners - 2, parts)[0], "cell", outer_groups)
    parts = exchange(add_blocks(1, outer, owners - 2, parts[:, None])[:, 0], "cell", outer_groups)
    return exchange(repeat(INNER, parts).reshape(blocks.shape), "cell", inner_groups)


def body(block_values, block_ids, block_count, cell_factor, gene_factor):
    values = block_values[0, 0]
    ids = block_ids[0, 0]
    count = block_count[0]
    rows = cell_factor.shape[0]
    n_cell, n_gene = lax.axis_size("cell"), lax.axis_size("gene")
    scale = (rows * n_cell) ** (-0.5)
    cell_share = rows // n_gene

    sums = across_cells(first_pass(scale, ids, count, values, cell_factor, gene_factor))
    new_genes, cell_terms = second_pass(scale, n_gene, ids, count, values, cell_factor, gene_factor, sums)
    cell_sums = exchange(add_cells(exchange(cell_terms, "gene")), "gene")
    new_cells = make_new_cells(scale, cell_share, cell_factor, cell_sums)
    return new_cells, new_genes


def solution(mesh):
    return jax.shard_map(
        body,
        mesh=mesh,
        in_specs=(
            P("cell", "gene", None, None, None),
            P("cell", "gene", None),
            P("cell", "gene"),
            P("cell", None),
            P("gene", None),
        ),
        out_specs=(P("cell", None), P("gene", None)),
        check_vma=False,
    )
```

```python
import functools

import jax
import jax.numpy as jnp
from jax import lax
from jax.experimental import pallas as pl
from jax.experimental.pallas import tpu as pltpu
from jax.sharding import PartitionSpec as P

LAMBDA = 0.5
F32 = jnp.float32
BF16 = jnp.bfloat16
NN = (((1,), (0,)), ((), ()))
NT = (((1,), (1,)), ((), ()))
PARAMS = pltpu.CompilerParams(vmem_limit_bytes=48 * 1024 * 1024)
SMEM = pl.BlockSpec(memory_space=pltpu.SMEM)
VMEM = pl.BlockSpec(memory_space=pltpu.VMEM)
HBM = pl.BlockSpec(memory_space=pltpu.HBM)
FIRST_STAGES = (5, 10, 15)
AHEAD = 8
PIECES = 1
INNER = 8


def dot(a, b, dims=NN):
    return lax.dot_general(a, b, dims, preferred_element_type=F32)


def exact_dot(a, b):
    return lax.dot_general(a, b, NN, precision=lax.Precision.HIGHEST, preferred_element_type=F32)


def split(value):
    high = value.astype(BF16)
    return high, (value - high.astype(F32)).astype(BF16)


def split_dot(a, b):
    return dot(a[0], b[0]) + (dot(a[0], b[1]) + dot(a[1], b[0]))


def two_terms(value):
    high = value.astype(BF16).astype(F32)
    return jnp.concatenate([high, value - high], axis=0).astype(BF16)


def start_loads(sem, small, large):
    copies = [pltpu.make_async_copy(source, target, sem.at[i]) for i, (source, target) in enumerate(small)]
    source, target = large
    step = source.shape[0] // PIECES
    for i in range(PIECES):
        part = pl.ds(i * step, step)
        copies.append(pltpu.make_async_copy(source.at[part], target.at[part], sem.at[len(small) + i]))
    for copy in copies:
        copy.start()
    return copies[: len(small)], copies[len(small) :]


def fill_positions(ids_ref, count_ref, pos_ref):
    slots = ids_ref.shape[0]
    for i in range(pos_ref.shape[0]):
        pos_ref[i] = slots
    count = count_ref[0]
    for k in range(slots):
        pos_ref[ids_ref[k]] = jnp.where(k < count, k, slots)


def residual_pair(vals_ref, pos_ref, resid_ref, fit, first, gene_blocks, at):
    blk = vals_ref.shape[1]
    for c in range(fit.shape[0] // blk):
        for h in range(2):
            value = vals_ref[pos_ref[c * gene_blocks + first + h]].astype(F32)
            part = value - fit[c * blk : (c + 1) * blk, h * blk : (h + 1) * blk]
            to = pl.ds((at + h) * blk, blk)
            resid_ref[pl.ds(c * blk, blk), to] = jnp.where(value != 0.0, part, 0.0).astype(BF16)


def first_pass_kernel(
    scale,
    gene_blocks,
    ids_hbm,
    count_ref,
    vals_hbm,
    cell_hbm,
    gene_hbm,
    out_hbm,
    sem,
    out_sem,
    ids_ref,
    pos_ref,
    vals_ref,
    cell_ref,
    gene_ref,
    turned_ref,
    fit_ref,
    resid_ref,
    out_ref,
):
    blk = vals_ref.shape[1]
    rank = cell_ref.shape[1]
    small, values = start_loads(
        sem, [(ids_hbm, ids_ref), (cell_hbm, cell_ref), (gene_hbm, gene_ref)], (vals_hbm, vals_ref.at[: vals_hbm.shape[0]])
    )
    vals_ref[vals_hbm.shape[0]] = jnp.zeros(vals_ref.shape[1:], BF16)
    small[1].wait()
    scaled = cell_ref[...].astype(F32) * scale
    turned_ref[...] = scaled.T.astype(BF16)
    cell_ref[...] = scaled.astype(BF16)
    gram = dot(turned_ref[...], cell_ref[...])
    out_ref[gene_blocks] = two_terms(gram[: rank // 2, :])
    out_ref[gene_blocks + 1] = two_terms(gram[rank // 2 :, :])
    small[2].wait()

    def fit_of(pair):
        return dot(cell_ref[...], gene_ref[2 * pair * blk : 2 * (pair + 1) * blk, :], NT)

    ahead = fit_ref.shape[0]
    for pair in range(ahead):
        fit_ref[pair] = fit_of(pair)
    small[0].wait()
    fill_positions(ids_ref, count_ref, pos_ref)
    for copy in values:
        copy.wait()

    stores = []
    low = 0
    for high in FIRST_STAGES:
        for pair in range(low, high):
            fit = fit_ref[pair] if pair < ahead else fit_of(pair)
            residual_pair(vals_ref, pos_ref, resid_ref, fit, 2 * pair, gene_blocks, 2 * pair)
        terms = dot(turned_ref[...], resid_ref[:, 2 * low * blk : 2 * high * blk]).astype(BF16)
        for u in range(2 * (high - low)):
            out_ref[2 * low + u] = terms[:, u * blk : (u + 1) * blk]
        to = pl.ds(2 * low, 2 * (high - low) + (2 if high == FIRST_STAGES[-1] else 0))
        stores.append(pltpu.make_async_copy(out_ref.at[to], out_hbm.at[to], out_sem.at[len(stores)]))
        stores[-1].start()
        low = high
    for store in stores:
        store.wait()


def first_pass(scale, ids, count, values, cells, genes):
    slots, blk, _ = values.shape
    rows, rank = cells.shape
    gene_blocks = genes.shape[0] // blk
    return pl.pallas_call(
        functools.partial(first_pass_kernel, scale, gene_blocks),
        out_shape=jax.ShapeDtypeStruct((gene_blocks + 2, rank, blk), BF16),
        in_specs=[HBM, SMEM, HBM, HBM, HBM],
        out_specs=HBM,
        scratch_shapes=[
            pltpu.SemaphoreType.DMA((PIECES + 3,)),
            pltpu.SemaphoreType.DMA((len(FIRST_STAGES),)),
            pltpu.SMEM((slots,), jnp.int32),
            pltpu.SMEM((rows // blk * gene_blocks,), jnp.int32),
            pltpu.VMEM((slots + 1, blk, blk), BF16),
            pltpu.VMEM(cells.shape, BF16),
            pltpu.VMEM(genes.shape, BF16),
            pltpu.VMEM((rank, rows), BF16),
            pltpu.VMEM((AHEAD, rows, 2 * blk), F32),
            pltpu.VMEM((rows, genes.shape[0]), BF16),
            pltpu.VMEM((gene_blocks + 2, rank, blk), BF16),
        ],
        compiler_params=pltpu.CompilerParams(vmem_limit_bytes=63 * 1024 * 1024),
        name="first_pass",
    )(ids, count, values, cells, genes)


def total_of(parts_ref, slot, rows):
    total = parts_ref[0, slot, rows, :].astype(F32)
    for i in range(1, parts_ref.shape[0]):
        total = total + parts_ref[i, slot, rows, :].astype(F32)
    return total


def add_blocks_kernel(stage, gram_from, parts_ref, out_ref):
    parts, slots, height, _ = parts_ref.shape
    place = lax.axis_index("cell")
    outer = lax.axis_size("cell") // INNER
    first = (place % INNER) * outer + (place // INNER if stage else 0)
    step = height // 4
    for slot in range(slots):
        may_be_gram = stage or slot >= gram_from % outer
        if may_be_gram:
            whole = total_of(parts_ref, slot, pl.ds(0, height))
            is_gram = first + slot >= gram_from
            gram = two_terms(whole[: height // 2, :] + whole[height // 2 :, :]).astype(F32)
            whole = jnp.where(is_gram, gram, whole).astype(BF16)
            for i in range(out_ref.shape[0]):
                out_ref[i, slot] = whole
        else:
            for low in range(0, height, step):
                rows = pl.ds(low, step)
                out_ref[0, slot, rows, :] = total_of(parts_ref, slot, rows).astype(BF16)


def add_blocks(stage, copies, gram_from, parts):
    return pl.pallas_call(
        functools.partial(add_blocks_kernel, stage, gram_from),
        out_shape=jax.ShapeDtypeStruct((copies,) + parts.shape[1:], BF16),
        in_specs=[VMEM],
        out_specs=VMEM,
        compiler_params=PARAMS,
        name="add_blocks",
    )(parts)


def repeat_kernel(part_ref, out_ref):
    for slot in range(part_ref.shape[0]):
        block = part_ref[slot]
        for i in range(out_ref.shape[0]):
            out_ref[i, slot] = block


def repeat(copies, part):
    return pl.pallas_call(
        repeat_kernel,
        out_shape=jax.ShapeDtypeStruct((copies,) + part.shape, BF16),
        in_specs=[VMEM],
        out_specs=VMEM,
        compiler_params=PARAMS,
        name="repeat",
    )(part)


def add_cells_kernel(parts_ref, out_ref):
    value = parts_ref[0].astype(F32)
    for i in range(1, parts_ref.shape[0]):
        value = value + parts_ref[i].astype(F32)
    total = value.astype(BF16)
    for i in range(out_ref.shape[0]):
        out_ref[i] = total


def add_cells(parts):
    return pl.pallas_call(
        add_cells_kernel,
        out_shape=jax.ShapeDtypeStruct(parts.shape, BF16),
        in_specs=[VMEM],
        out_specs=VMEM,
        compiler_params=PARAMS,
        name="add_cells",
    )(parts)


def eliminate(work, row, column):
    for k in range(work.shape[0]):
        at_row = row[:, 0:1] == k
        at_column = column[0:1, :] == k
        line = work[k : k + 1, :]
        pivot = 1.0 / work[k : k + 1, k : k + 1]
        side = work[:, k : k + 1] - jnp.where(at_row, 1.0, 0.0)
        line = jnp.where(at_column, 1.0, line) * pivot
        kept = jnp.where(at_column, jnp.where(at_row, 1.0, 0.0), work)
        work = kept - side * line
    return work


def solve_into(solve_ref, inverse_ref, gram):
    rank = gram.shape[0]
    row = lax.broadcasted_iota(jnp.int32, (rank, rank), 0)
    column = lax.broadcasted_iota(jnp.int32, (rank, rank), 1)
    diagonal = row == column
    eye = jnp.where(diagonal, 1.0, 0.0)
    matrix = gram + LAMBDA * eye
    along = jnp.where(diagonal, matrix, 0.0)
    down = 1.0 / jnp.sum(along, axis=1, keepdims=True)
    across = 1.0 / jnp.sum(along, axis=0, keepdims=True)
    off = (eye - matrix * across).astype(BF16)
    guess = (eye + (eye - matrix * across)) * down
    guess = guess + dot(guess.astype(BF16), dot(off, off).astype(BF16))
    rest = eye - exact_dot(matrix, guess)
    inverse_ref[...] = guess + split_dot(split(guess), split(rest))
    size = jnp.sum(rest * rest)

    @pl.when(jnp.logical_not(size < 4e-6))
    def _():
        inverse_ref[...] = eliminate(matrix, row, column)

    inverse = inverse_ref[...]
    high, low = split(inverse)
    first, second = split(split_dot((high, low), split(gram)))
    solve_ref[:, 0:rank] = first
    solve_ref[:, rank : 2 * rank] = second
    solve_ref[:, 2 * rank : 3 * rank] = high
    solve_ref[:, 3 * rank : 4 * rank] = low


def second_pass_kernel(
    scale,
    ids_hbm,
    count_ref,
    vals_hbm,
    cell_hbm,
    gene_hbm,
    sums_ref,
    new_hbm,
    out_ref,
    sem,
    out_sem,
    ids_ref,
    pos_ref,
    vals_ref,
    cell_ref,
    gene_ref,
    solve_ref,
    new_ref,
    turned_ref,
    resid_ref,
    total_ref,
):
    blk = vals_ref.shape[1]
    rank = cell_ref.shape[1]
    gene_blocks = gene_ref.shape[0] // blk
    small, values = start_loads(
        sem, [(ids_hbm, ids_ref), (cell_hbm, cell_ref), (gene_hbm, gene_ref)], (vals_hbm, vals_ref.at[: vals_hbm.shape[0]])
    )
    vals_ref[vals_hbm.shape[0]] = jnp.zeros(vals_ref.shape[1:], BF16)
    small[0].wait()
    fill_positions(ids_ref, count_ref, pos_ref)
    halves = [sums_ref[gene_blocks + i].astype(F32) for i in range(2)]
    gram = jnp.concatenate([half[: rank // 2, :] + half[rank // 2 :, :] for half in halves], axis=0)
    solve_into(solve_ref, total_ref.at[:rank, :], gram)
    for copy in small[1:]:
        copy.wait()
    cell_ref[...] = (cell_ref[...].astype(F32) * scale).astype(BF16)
    pairs = gene_blocks // 2
    for pair in range(pairs):
        rows = pl.ds(2 * pair * blk, 2 * blk)
        sums = jnp.concatenate([sums_ref[2 * pair], sums_ref[2 * pair + 1]], axis=1)
        old = gene_ref[rows, :]
        turned = (
            dot(solve_ref[:, 0:rank], old, NT)
            + dot(solve_ref[:, rank : 2 * rank], old, NT)
            + dot(solve_ref[:, 2 * rank : 4 * rank], jnp.concatenate([sums, sums], axis=0))
        )
        new_ref[rows, :] = turned.T.astype(BF16)
        turned_ref[:, rows] = turned.astype(BF16)
    store = pltpu.make_async_copy(new_ref, new_hbm, out_sem)
    store.start()
    gram = dot(turned_ref[...], new_ref[...])
    for copy in values:
        copy.wait()
    for pair in range(pairs):
        genes = new_ref[2 * pair * blk : 2 * (pair + 1) * blk, :]
        residual_pair(vals_ref, pos_ref, resid_ref, dot(cell_ref[...], genes, NT), 2 * pair, gene_blocks, 2 * pair)
    total_ref[...] = dot(resid_ref[...], new_ref[...])
    owners, out_height, _ = out_ref.shape
    count = total_ref.shape[0] // owners
    lines = out_height - count
    for i in range(owners):
        out_ref[i, :count, :] = total_ref[i * count : (i + 1) * count, :].astype(BF16)
        out_ref[i, count:, :] = gram[i * lines : (i + 1) * lines, :].astype(BF16)
    store.wait()


def second_pass(scale, owners, ids, count, values, cells, genes, sums):
    slots, blk, _ = values.shape
    rows, rank = cells.shape
    gene_blocks = genes.shape[0] // blk
    height = (rows + rank) // owners
    return pl.pallas_call(
        functools.partial(second_pass_kernel, scale),
        out_shape=(jax.ShapeDtypeStruct(genes.shape, BF16), jax.ShapeDtypeStruct((owners, height, rank), BF16)),
        in_specs=[HBM, SMEM, HBM, HBM, HBM, VMEM],
        out_specs=(HBM, VMEM),
        scratch_shapes=[
            pltpu.SemaphoreType.DMA((PIECES + 3,)),
            pltpu.SemaphoreType.DMA,
            pltpu.SMEM((slots,), jnp.int32),
            pltpu.SMEM((rows // blk * gene_blocks,), jnp.int32),
            pltpu.VMEM((slots + 1, blk, blk), BF16),
            pltpu.VMEM(cells.shape, BF16),
            pltpu.VMEM(genes.shape, BF16),
            pltpu.VMEM((rank, 4 * rank), BF16),
            pltpu.VMEM(genes.shape, BF16),
            pltpu.VMEM((rank, genes.shape[0]), BF16),
            pltpu.VMEM((rows, genes.shape[0]), BF16),
            pltpu.VMEM((rows, rank), F32),
        ],
        compiler_params=PARAMS,
        name="second_pass",
    )(ids, count, values, cells, genes, sums)


def new_cells_kernel(scale, share, cell_ref, sums_ref, out_ref, solve_ref, gram_ref, inverse_ref):
    rank = cell_ref.shape[1]
    senders, height, _ = sums_ref.shape
    lines = height - share
    for i in range(senders):
        gram_ref[i * lines : (i + 1) * lines, :] = sums_ref[i, share:, :].astype(F32)
    solve_into(solve_ref, inverse_ref, gram_ref[...])
    sums = (sums_ref[:, :share, :].reshape(senders * share, rank).astype(F32) * (1.0 / scale)).astype(BF16)
    out_ref[...] = (
        dot(cell_ref[...], solve_ref[:, 0:rank], NT)
        + dot(cell_ref[...], solve_ref[:, rank : 2 * rank], NT)
        + dot(sums, solve_ref[:, 2 * rank : 3 * rank], NT)
        + dot(sums, solve_ref[:, 3 * rank : 4 * rank], NT)
    ).astype(BF16)


def make_new_cells(scale, share, cells, sums):
    rank = cells.shape[1]
    return pl.pallas_call(
        functools.partial(new_cells_kernel, scale, share),
        out_shape=jax.ShapeDtypeStruct(cells.shape, BF16),
        in_specs=[VMEM] * 2,
        out_specs=VMEM,
        scratch_shapes=[
            pltpu.VMEM((rank, 4 * rank), BF16),
            pltpu.VMEM((rank, rank), F32),
            pltpu.VMEM((rank, rank), F32),
        ],
        compiler_params=PARAMS,
        name="new_cells",
    )(cells, sums)


def exchange(parts, axis, groups=None):
    return lax.all_to_all(parts, axis, 0, 0, tiled=True, axis_index_groups=groups)


def across_cells(blocks):
    owners = blocks.shape[0]
    outer = owners // INNER
    inner_groups = [[o * INNER + i for i in range(INNER)] for o in range(outer)]
    outer_groups = [[o * INNER + i for o in range(outer)] for i in range(INNER)]
    parts = exchange(blocks, "cell", inner_groups).reshape((INNER, outer) + blocks.shape[1:])
    parts = exchange(add_blocks(0, 1, owners - 2, parts)[0], "cell", outer_groups)
    parts = exchange(add_blocks(1, outer, owners - 2, parts[:, None])[:, 0], "cell", outer_groups)
    return exchange(repeat(INNER, parts).reshape(blocks.shape), "cell", inner_groups)


def body(block_values, block_ids, block_count, cell_factor, gene_factor):
    values = block_values[0, 0]
    ids = block_ids[0, 0]
    count = block_count[0]
    rows = cell_factor.shape[0]
    n_cell, n_gene = lax.axis_size("cell"), lax.axis_size("gene")
    scale = (rows * n_cell) ** (-0.5)
    cell_share = rows // n_gene

    sums = across_cells(first_pass(scale, ids, count, values, cell_factor, gene_factor))
    new_genes, cell_terms = second_pass(scale, n_gene, ids, count, values, cell_factor, gene_factor, sums)
    cell_sums = exchange(add_cells(exchange(cell_terms, "gene")), "gene")
    new_cells = make_new_cells(scale, cell_share, cell_factor, cell_sums)
    return new_cells, new_genes


def solution(mesh):
    return jax.shard_map(
        body,
        mesh=mesh,
        in_specs=(
            P("cell", "gene", None, None, None),
            P("cell", "gene", None),
            P("cell", "gene"),
            P("cell", None),
            P("gene", None),
        ),
        out_specs=(P("cell", None), P("gene", None)),
        check_vma=False,
    )
```

```python
import functools

import jax
import jax.numpy as jnp
from jax import lax
from jax.experimental import pallas as pl
from jax.experimental.pallas import tpu as pltpu
from jax.sharding import PartitionSpec as P

LAMBDA = 0.5
F32 = jnp.float32
BF16 = jnp.bfloat16
NN = (((1,), (0,)), ((), ()))
NT = (((1,), (1,)), ((), ()))
PARAMS = pltpu.CompilerParams(vmem_limit_bytes=48 * 1024 * 1024)
SMEM = pl.BlockSpec(memory_space=pltpu.SMEM)
VMEM = pl.BlockSpec(memory_space=pltpu.VMEM)
HBM = pl.BlockSpec(memory_space=pltpu.HBM)
FIRST_STAGES = (5, 10, 15)
AHEAD = 8
PIECES = 1
INNER = 8


def dot(a, b, dims=NN):
    return lax.dot_general(a, b, dims, preferred_element_type=F32)


def exact_dot(a, b):
    return lax.dot_general(a, b, NN, precision=lax.Precision.HIGHEST, preferred_element_type=F32)


def split(value):
    high = value.astype(BF16)
    return high, (value - high.astype(F32)).astype(BF16)


def split_dot(a, b):
    return dot(a[0], b[0]) + (dot(a[0], b[1]) + dot(a[1], b[0]))


def two_terms(value):
    high = value.astype(BF16).astype(F32)
    return jnp.concatenate([high, value - high], axis=0).astype(BF16)


def start_loads(sem, small, large):
    copies = [pltpu.make_async_copy(source, target, sem.at[i]) for i, (source, target) in enumerate(small)]
    source, target = large
    step = source.shape[0] // PIECES
    for i in range(PIECES):
        part = pl.ds(i * step, step)
        copies.append(pltpu.make_async_copy(source.at[part], target.at[part], sem.at[len(small) + i]))
    for copy in copies:
        copy.start()
    return copies[: len(small)], copies[len(small) :]


def fill_positions(ids_ref, count_ref, pos_ref):
    slots = ids_ref.shape[0]
    for i in range(pos_ref.shape[0]):
        pos_ref[i] = slots
    count = count_ref[0]
    for k in range(slots):
        pos_ref[ids_ref[k]] = jnp.where(k < count, k, slots)


def residual_pair(vals_ref, pos_ref, resid_ref, fit, first, gene_blocks, at):
    blk = vals_ref.shape[1]
    for c in range(fit.shape[0] // blk):
        for h in range(2):
            value = vals_ref[pos_ref[c * gene_blocks + first + h]].astype(F32)
            part = value - fit[c * blk : (c + 1) * blk, h * blk : (h + 1) * blk]
            to = pl.ds((at + h) * blk, blk)
            resid_ref[pl.ds(c * blk, blk), to] = jnp.where(value != 0.0, part, 0.0).astype(BF16)


def first_pass_kernel(
    scale,
    gene_blocks,
    ids_hbm,
    count_ref,
    vals_hbm,
    cell_hbm,
    gene_hbm,
    out_hbm,
    sem,
    out_sem,
    ids_ref,
    pos_ref,
    vals_ref,
    cell_ref,
    gene_ref,
    turned_ref,
    fit_ref,
    resid_ref,
    out_ref,
):
    blk = vals_ref.shape[1]
    rank = cell_ref.shape[1]
    small, values = start_loads(
        sem, [(ids_hbm, ids_ref), (cell_hbm, cell_ref), (gene_hbm, gene_ref)], (vals_hbm, vals_ref.at[: vals_hbm.shape[0]])
    )
    vals_ref[vals_hbm.shape[0]] = jnp.zeros(vals_ref.shape[1:], BF16)
    small[1].wait()
    scaled = cell_ref[...].astype(F32) * scale
    turned_ref[...] = scaled.T.astype(BF16)
    cell_ref[...] = scaled.astype(BF16)
    gram = dot(turned_ref[...], cell_ref[...])
    out_ref[gene_blocks] = two_terms(gram[: rank // 2, :])
    out_ref[gene_blocks + 1] = two_terms(gram[rank // 2 :, :])
    small[2].wait()

    def fit_of(pair):
        return dot(cell_ref[...], gene_ref[2 * pair * blk : 2 * (pair + 1) * blk, :], NT)

    ahead = fit_ref.shape[0]
    for pair in range(ahead):
        fit_ref[pair] = fit_of(pair)
    small[0].wait()
    fill_positions(ids_ref, count_ref, pos_ref)
    for copy in values:
        copy.wait()

    stores = []
    low = 0
    for high in FIRST_STAGES:
        for pair in range(low, high):
            fit = fit_ref[pair] if pair < ahead else fit_of(pair)
            residual_pair(vals_ref, pos_ref, resid_ref, fit, 2 * pair, gene_blocks, 2 * pair)
        terms = dot(turned_ref[...], resid_ref[:, 2 * low * blk : 2 * high * blk]).astype(BF16)
        for u in range(2 * (high - low)):
            out_ref[2 * low + u] = terms[:, u * blk : (u + 1) * blk]
        to = pl.ds(2 * low, 2 * (high - low) + (2 if high == FIRST_STAGES[-1] else 0))
        stores.append(pltpu.make_async_copy(out_ref.at[to], out_hbm.at[to], out_sem.at[len(stores)]))
        stores[-1].start()
        low = high
    for store in stores:
        store.wait()


def first_pass(scale, ids, count, values, cells, genes):
    slots, blk, _ = values.shape
    rows, rank = cells.shape
    gene_blocks = genes.shape[0] // blk
    return pl.pallas_call(
        functools.partial(first_pass_kernel, scale, gene_blocks),
        out_shape=jax.ShapeDtypeStruct((gene_blocks + 2, rank, blk), BF16),
        in_specs=[HBM, SMEM, HBM, HBM, HBM],
        out_specs=HBM,
        scratch_shapes=[
            pltpu.SemaphoreType.DMA((PIECES + 3,)),
            pltpu.SemaphoreType.DMA((len(FIRST_STAGES),)),
            pltpu.SMEM((slots,), jnp.int32),
            pltpu.SMEM((rows // blk * gene_blocks,), jnp.int32),
            pltpu.VMEM((slots + 1, blk, blk), BF16),
            pltpu.VMEM(cells.shape, BF16),
            pltpu.VMEM(genes.shape, BF16),
            pltpu.VMEM((rank, rows), BF16),
            pltpu.VMEM((AHEAD, rows, 2 * blk), F32),
            pltpu.VMEM((rows, genes.shape[0]), BF16),
            pltpu.VMEM((gene_blocks + 2, rank, blk), BF16),
        ],
        compiler_params=pltpu.CompilerParams(vmem_limit_bytes=63 * 1024 * 1024),
        name="first_pass",
    )(ids, count, values, cells, genes)


def total_of(parts_ref, slot, rows):
    total = parts_ref[0, slot, rows, :].astype(F32)
    for i in range(1, parts_ref.shape[0]):
        total = total + parts_ref[i, slot, rows, :].astype(F32)
    return total


def add_blocks_kernel(stage, gram_from, parts_ref, out_ref):
    parts, slots, height, _ = parts_ref.shape
    place = lax.axis_index("cell")
    outer = lax.axis_size("cell") // INNER
    first = (place % INNER) * outer + (place // INNER if stage else 0)
    step = height // 4
    for slot in range(slots):
        may_be_gram = stage or slot >= gram_from % outer
        if may_be_gram:
            whole = total_of(parts_ref, slot, pl.ds(0, height))
            is_gram = first + slot >= gram_from
            gram = two_terms(whole[: height // 2, :] + whole[height // 2 :, :]).astype(F32)
            whole = jnp.where(is_gram, gram, whole).astype(BF16)
            for i in range(out_ref.shape[0]):
                out_ref[i, slot] = whole
        else:
            for low in range(0, height, step):
                rows = pl.ds(low, step)
                out_ref[0, slot, rows, :] = total_of(parts_ref, slot, rows).astype(BF16)


def add_blocks(stage, copies, gram_from, parts):
    return pl.pallas_call(
        functools.partial(add_blocks_kernel, stage, gram_from),
        out_shape=jax.ShapeDtypeStruct((copies,) + parts.shape[1:], BF16),
        in_specs=[VMEM],
        out_specs=VMEM,
        compiler_params=PARAMS,
        name="add_blocks",
    )(parts)


def repeat_kernel(part_ref, out_ref):
    for slot in range(part_ref.shape[0]):
        block = part_ref[slot]
        for i in range(out_ref.shape[0]):
            out_ref[i, slot] = block


def repeat(copies, part):
    return pl.pallas_call(
        repeat_kernel,
        out_shape=jax.ShapeDtypeStruct((copies,) + part.shape, BF16),
        in_specs=[VMEM],
        out_specs=VMEM,
        compiler_params=PARAMS,
        name="repeat",
    )(part)


def add_cells_kernel(parts_ref, out_ref):
    value = parts_ref[0].astype(F32)
    for i in range(1, parts_ref.shape[0]):
        value = value + parts_ref[i].astype(F32)
    total = value.astype(BF16)
    for i in range(out_ref.shape[0]):
        out_ref[i] = total


def add_cells(parts):
    return pl.pallas_call(
        add_cells_kernel,
        out_shape=jax.ShapeDtypeStruct(parts.shape, BF16),
        in_specs=[VMEM],
        out_specs=VMEM,
        compiler_params=PARAMS,
        name="add_cells",
    )(parts)


def eliminate(work, row, column):
    for k in range(work.shape[0]):
        at_row = row[:, 0:1] == k
        at_column = column[0:1, :] == k
        line = work[k : k + 1, :]
        pivot = 1.0 / work[k : k + 1, k : k + 1]
        side = work[:, k : k + 1] - jnp.where(at_row, 1.0, 0.0)
        line = jnp.where(at_column, 1.0, line) * pivot
        kept = jnp.where(at_column, jnp.where(at_row, 1.0, 0.0), work)
        work = kept - side * line
    return work


def solve_into(solve_ref, inverse_ref, gram):
    rank = gram.shape[0]
    row = lax.broadcasted_iota(jnp.int32, (rank, rank), 0)
    column = lax.broadcasted_iota(jnp.int32, (rank, rank), 1)
    diagonal = row == column
    eye = jnp.where(diagonal, 1.0, 0.0)
    matrix = gram + LAMBDA * eye
    along = jnp.where(diagonal, matrix, 0.0)
    down = 1.0 / jnp.sum(along, axis=1, keepdims=True)
    across = 1.0 / jnp.sum(along, axis=0, keepdims=True)
    off = (eye - matrix * across).astype(BF16)
    guess = (eye + (eye - matrix * across)) * down
    guess = guess + dot(guess.astype(BF16), dot(off, off).astype(BF16))
    rest = eye - exact_dot(matrix, guess)
    inverse_ref[...] = guess + split_dot(split(guess), split(rest))
    size = jnp.sum(rest * rest)

    @pl.when(jnp.logical_not(size < 4e-6))
    def _():
        inverse_ref[...] = eliminate(matrix, row, column)

    inverse = inverse_ref[...]
    high, low = split(inverse)
    first, second = split(split_dot((high, low), split(gram)))
    solve_ref[:, 0:rank] = first
    solve_ref[:, rank : 2 * rank] = second
    solve_ref[:, 2 * rank : 3 * rank] = high
    solve_ref[:, 3 * rank : 4 * rank] = low


def second_pass_kernel(
    scale,
    ids_hbm,
    count_ref,
    vals_hbm,
    cell_hbm,
    gene_hbm,
    sums_ref,
    new_hbm,
    out_ref,
    sem,
    out_sem,
    ids_ref,
    pos_ref,
    vals_ref,
    cell_ref,
    gene_ref,
    solve_ref,
    new_ref,
    turned_ref,
    resid_ref,
    total_ref,
):
    blk = vals_ref.shape[1]
    rank = cell_ref.shape[1]
    gene_blocks = gene_ref.shape[0] // blk
    small, values = start_loads(
        sem, [(ids_hbm, ids_ref), (cell_hbm, cell_ref), (gene_hbm, gene_ref)], (vals_hbm, vals_ref.at[: vals_hbm.shape[0]])
    )
    vals_ref[vals_hbm.shape[0]] = jnp.zeros(vals_ref.shape[1:], BF16)
    small[0].wait()
    fill_positions(ids_ref, count_ref, pos_ref)
    halves = [sums_ref[gene_blocks + i].astype(F32) for i in range(2)]
    gram = jnp.concatenate([half[: rank // 2, :] + half[rank // 2 :, :] for half in halves], axis=0)
    solve_into(solve_ref, total_ref.at[:rank, :], gram)
    for copy in small[1:]:
        copy.wait()
    cell_ref[...] = (cell_ref[...].astype(F32) * scale).astype(BF16)
    pairs = gene_blocks // 2
    for pair in range(pairs):
        rows = pl.ds(2 * pair * blk, 2 * blk)
        sums = jnp.concatenate([sums_ref[2 * pair], sums_ref[2 * pair + 1]], axis=1)
        old = gene_ref[rows, :]
        turned = (
            dot(solve_ref[:, 0:rank], old, NT)
            + dot(solve_ref[:, rank : 2 * rank], old, NT)
            + dot(solve_ref[:, 2 * rank : 4 * rank], jnp.concatenate([sums, sums], axis=0))
        )
        new_ref[rows, :] = turned.T.astype(BF16)
        turned_ref[:, rows] = turned.astype(BF16)
    store = pltpu.make_async_copy(new_ref, new_hbm, out_sem)
    store.start()
    gram = dot(turned_ref[...], new_ref[...])
    for copy in values:
        copy.wait()
    for pair in range(pairs):
        genes = new_ref[2 * pair * blk : 2 * (pair + 1) * blk, :]
        residual_pair(vals_ref, pos_ref, resid_ref, dot(cell_ref[...], genes, NT), 2 * pair, gene_blocks, 2 * pair)
    total_ref[...] = dot(resid_ref[...], new_ref[...])
    owners, out_height, _ = out_ref.shape
    count = total_ref.shape[0] // owners
    lines = out_height - count
    for i in range(owners):
        out_ref[i, :count, :] = total_ref[i * count : (i + 1) * count, :].astype(BF16)
        out_ref[i, count:, :] = gram[i * lines : (i + 1) * lines, :].astype(BF16)
    store.wait()


def second_pass(scale, owners, ids, count, values, cells, genes, sums):
    slots, blk, _ = values.shape
    rows, rank = cells.shape
    gene_blocks = genes.shape[0] // blk
    height = (rows + rank) // owners
    return pl.pallas_call(
        functools.partial(second_pass_kernel, scale),
        out_shape=(jax.ShapeDtypeStruct(genes.shape, BF16), jax.ShapeDtypeStruct((owners, height, rank), BF16)),
        in_specs=[HBM, SMEM, HBM, HBM, HBM, VMEM],
        out_specs=(HBM, VMEM),
        scratch_shapes=[
            pltpu.SemaphoreType.DMA((PIECES + 3,)),
            pltpu.SemaphoreType.DMA,
            pltpu.SMEM((slots,), jnp.int32),
            pltpu.SMEM((rows // blk * gene_blocks,), jnp.int32),
            pltpu.VMEM((slots + 1, blk, blk), BF16),
            pltpu.VMEM(cells.shape, BF16),
            pltpu.VMEM(genes.shape, BF16),
            pltpu.VMEM((rank, 4 * rank), BF16),
            pltpu.VMEM(genes.shape, BF16),
            pltpu.VMEM((rank, genes.shape[0]), BF16),
            pltpu.VMEM((rows, genes.shape[0]), BF16),
            pltpu.VMEM((rows, rank), F32),
        ],
        compiler_params=PARAMS,
        name="second_pass",
    )(ids, count, values, cells, genes, sums)


def new_cells_kernel(scale, share, cell_ref, sums_ref, out_ref, solve_ref, gram_ref, inverse_ref):
    rank = cell_ref.shape[1]
    senders, height, _ = sums_ref.shape
    lines = height - share
    for i in range(senders):
        gram_ref[i * lines : (i + 1) * lines, :] = sums_ref[i, share:, :].astype(F32)
    solve_into(solve_ref, inverse_ref, gram_ref[...])
    sums = (sums_ref[:, :share, :].reshape(senders * share, rank).astype(F32) * (1.0 / scale)).astype(BF16)
    out_ref[...] = (
        dot(jnp.concatenate([cell_ref[...]] * 2, axis=1), solve_ref[:, 0 : 2 * rank], NT)
        + dot(jnp.concatenate([sums] * 2, axis=1), solve_ref[:, 2 * rank : 4 * rank], NT)
    ).astype(BF16)


def make_new_cells(scale, share, cells, sums):
    rank = cells.shape[1]
    return pl.pallas_call(
        functools.partial(new_cells_kernel, scale, share),
        out_shape=jax.ShapeDtypeStruct(cells.shape, BF16),
        in_specs=[VMEM] * 2,
        out_specs=VMEM,
        scratch_shapes=[
            pltpu.VMEM((rank, 4 * rank), BF16),
            pltpu.VMEM((rank, rank), F32),
            pltpu.VMEM((rank, rank), F32),
        ],
        compiler_params=PARAMS,
        name="new_cells",
    )(cells, sums)


def exchange(parts, axis, groups=None):
    return lax.all_to_all(parts, axis, 0, 0, tiled=True, axis_index_groups=groups)


def across_cells(blocks):
    owners = blocks.shape[0]
    outer = owners // INNER
    inner_groups = [[o * INNER + i for i in range(INNER)] for o in range(outer)]
    outer_groups = [[o * INNER + i for o in range(outer)] for i in range(INNER)]
    parts = exchange(blocks, "cell", inner_groups).reshape((INNER, outer) + blocks.shape[1:])
    parts = exchange(add_blocks(0, 1, owners - 2, parts)[0], "cell", outer_groups)
    parts = exchange(add_blocks(1, outer, owners - 2, parts[:, None])[:, 0], "cell", outer_groups)
    return exchange(repeat(INNER, parts).reshape(blocks.shape), "cell", inner_groups)


def body(block_values, block_ids, block_count, cell_factor, gene_factor):
    values = block_values[0, 0]
    ids = block_ids[0, 0]
    count = block_count[0]
    rows = cell_factor.shape[0]
    n_cell, n_gene = lax.axis_size("cell"), lax.axis_size("gene")
    scale = (rows * n_cell) ** (-0.5)
    cell_share = rows // n_gene

    sums = across_cells(first_pass(scale, ids, count, values, cell_factor, gene_factor))
    new_genes, cell_terms = second_pass(scale, n_gene, ids, count, values, cell_factor, gene_factor, sums)
    cell_sums = exchange(add_cells(exchange(cell_terms, "gene")), "gene")
    new_cells = make_new_cells(scale, cell_share, cell_factor, cell_sums)
    return new_cells, new_genes


def solution(mesh):
    return jax.shard_map(
        body,
        mesh=mesh,
        in_specs=(
            P("cell", "gene", None, None, None),
            P("cell", "gene", None),
            P("cell", "gene"),
            P("cell", None),
            P("gene", None),
        ),
        out_specs=(P("cell", None), P("gene", None)),
        check_vma=False,
    )
```

```python
import functools

import jax
import jax.numpy as jnp
from jax import lax
from jax.experimental import pallas as pl
from jax.experimental.pallas import tpu as pltpu
from jax.sharding import PartitionSpec as P

LAMBDA = 0.5
F32 = jnp.float32
BF16 = jnp.bfloat16
NN = (((1,), (0,)), ((), ()))
NT = (((1,), (1,)), ((), ()))
PARAMS = pltpu.CompilerParams(vmem_limit_bytes=48 * 1024 * 1024)
SMEM = pl.BlockSpec(memory_space=pltpu.SMEM)
VMEM = pl.BlockSpec(memory_space=pltpu.VMEM)
HBM = pl.BlockSpec(memory_space=pltpu.HBM)
FIRST_STAGES = (5, 10, 15)
AHEAD = 6
PIECES = 1
INNER = 8


def dot(a, b, dims=NN):
    return lax.dot_general(a, b, dims, preferred_element_type=F32)


def exact_dot(a, b):
    return lax.dot_general(a, b, NN, precision=lax.Precision.HIGHEST, preferred_element_type=F32)


def split(value):
    high = value.astype(BF16)
    return high, (value - high.astype(F32)).astype(BF16)


def split_dot(a, b):
    return dot(a[0], b[0]) + (dot(a[0], b[1]) + dot(a[1], b[0]))


def two_terms(value):
    high = value.astype(BF16).astype(F32)
    return jnp.concatenate([high, value - high], axis=0).astype(BF16)


def start_loads(sem, small, large):
    copies = [pltpu.make_async_copy(source, target, sem.at[i]) for i, (source, target) in enumerate(small)]
    source, target = large
    step = source.shape[0] // PIECES
    for i in range(PIECES):
        part = pl.ds(i * step, step)
        copies.append(pltpu.make_async_copy(source.at[part], target.at[part], sem.at[len(small) + i]))
    for copy in copies:
        copy.start()
    return copies[: len(small)], copies[len(small) :]


def fill_positions(ids_ref, count_ref, pos_ref):
    slots = ids_ref.shape[0]
    for i in range(pos_ref.shape[0]):
        pos_ref[i] = slots
    count = count_ref[0]
    for k in range(slots):
        pos_ref[ids_ref[k]] = jnp.where(k < count, k, slots)


def residual_pair(vals_ref, pos_ref, resid_ref, fit, first, gene_blocks, at):
    blk = vals_ref.shape[1]
    for c in range(fit.shape[0] // blk):
        for h in range(2):
            value = vals_ref[pos_ref[c * gene_blocks + first + h]].astype(F32)
            part = value - fit[c * blk : (c + 1) * blk, h * blk : (h + 1) * blk]
            to = pl.ds((at + h) * blk, blk)
            resid_ref[pl.ds(c * blk, blk), to] = jnp.where(value != 0.0, part, 0.0).astype(BF16)


def first_pass_kernel(
    scale,
    gene_blocks,
    ids_hbm,
    count_ref,
    vals_hbm,
    cell_hbm,
    gene_hbm,
    out_hbm,
    sem,
    out_sem,
    ids_ref,
    pos_ref,
    vals_ref,
    cell_ref,
    gene_ref,
    turned_ref,
    fit_ref,
    resid_ref,
    out_ref,
):
    blk = vals_ref.shape[1]
    rank = cell_ref.shape[1]
    small, values = start_loads(
        sem, [(ids_hbm, ids_ref), (cell_hbm, cell_ref), (gene_hbm, gene_ref)], (vals_hbm, vals_ref.at[: vals_hbm.shape[0]])
    )
    vals_ref[vals_hbm.shape[0]] = jnp.zeros(vals_ref.shape[1:], BF16)
    small[1].wait()
    scaled = cell_ref[...].astype(F32) * scale
    turned_ref[...] = scaled.T.astype(BF16)
    cell_ref[...] = scaled.astype(BF16)
    gram = dot(turned_ref[...], cell_ref[...])
    out_ref[gene_blocks] = two_terms(gram[: rank // 2, :])
    out_ref[gene_blocks + 1] = two_terms(gram[rank // 2 :, :])
    small[2].wait()

    def fit_of(pair):
        return dot(cell_ref[...], gene_ref[2 * pair * blk : 2 * (pair + 1) * blk, :], NT)

    ahead = fit_ref.shape[0]
    for pair in range(ahead):
        fit_ref[pair] = fit_of(pair)
    small[0].wait()
    fill_positions(ids_ref, count_ref, pos_ref)
    for copy in values:
        copy.wait()

    stores = []
    low = 0
    for high in FIRST_STAGES:
        for pair in range(low, high):
            fit = fit_ref[pair] if pair < ahead else fit_of(pair)
            residual_pair(vals_ref, pos_ref, resid_ref, fit, 2 * pair, gene_blocks, 2 * pair)
        terms = dot(turned_ref[...], resid_ref[:, 2 * low * blk : 2 * high * blk]).astype(BF16)
        for u in range(2 * (high - low)):
            out_ref[2 * low + u] = terms[:, u * blk : (u + 1) * blk]
        to = pl.ds(2 * low, 2 * (high - low) + (2 if high == FIRST_STAGES[-1] else 0))
        stores.append(pltpu.make_async_copy(out_ref.at[to], out_hbm.at[to], out_sem.at[len(stores)]))
        stores[-1].start()
        low = high
    for store in stores:
        store.wait()


def first_pass(scale, ids, count, values, cells, genes):
    slots, blk, _ = values.shape
    rows, rank = cells.shape
    gene_blocks = genes.shape[0] // blk
    return pl.pallas_call(
        functools.partial(first_pass_kernel, scale, gene_blocks),
        out_shape=jax.ShapeDtypeStruct((gene_blocks + 2, rank, blk), BF16),
        in_specs=[HBM, SMEM, HBM, HBM, HBM],
        out_specs=HBM,
        scratch_shapes=[
            pltpu.SemaphoreType.DMA((PIECES + 3,)),
            pltpu.SemaphoreType.DMA((len(FIRST_STAGES),)),
            pltpu.SMEM((slots,), jnp.int32),
            pltpu.SMEM((rows // blk * gene_blocks,), jnp.int32),
            pltpu.VMEM((slots + 1, blk, blk), BF16),
            pltpu.VMEM(cells.shape, BF16),
            pltpu.VMEM(genes.shape, BF16),
            pltpu.VMEM((rank, rows), BF16),
            pltpu.VMEM((AHEAD, rows, 2 * blk), F32),
            pltpu.VMEM((rows, genes.shape[0]), BF16),
            pltpu.VMEM((gene_blocks + 2, rank, blk), BF16),
        ],
        compiler_params=pltpu.CompilerParams(vmem_limit_bytes=63 * 1024 * 1024),
        name="first_pass",
    )(ids, count, values, cells, genes)


def total_of(parts_ref, slot, rows):
    total = parts_ref[0, slot, rows, :].astype(F32)
    for i in range(1, parts_ref.shape[0]):
        total = total + parts_ref[i, slot, rows, :].astype(F32)
    return total


def add_blocks_kernel(stage, gram_from, parts_ref, out_ref):
    parts, slots, height, _ = parts_ref.shape
    place = lax.axis_index("cell")
    outer = lax.axis_size("cell") // INNER
    first = (place % INNER) * outer + (place // INNER if stage else 0)
    step = height // 4
    for slot in range(slots):
        may_be_gram = stage or slot >= gram_from % outer
        if may_be_gram:
            whole = total_of(parts_ref, slot, pl.ds(0, height))
            is_gram = first + slot >= gram_from
            gram = two_terms(whole[: height // 2, :] + whole[height // 2 :, :]).astype(F32)
            whole = jnp.where(is_gram, gram, whole).astype(BF16)
            for i in range(out_ref.shape[0]):
                out_ref[i, slot] = whole
        else:
            for low in range(0, height, step):
                rows = pl.ds(low, step)
                out_ref[0, slot, rows, :] = total_of(parts_ref, slot, rows).astype(BF16)


def add_blocks(stage, copies, gram_from, parts):
    return pl.pallas_call(
        functools.partial(add_blocks_kernel, stage, gram_from),
        out_shape=jax.ShapeDtypeStruct((copies,) + parts.shape[1:], BF16),
        in_specs=[VMEM],
        out_specs=VMEM,
        compiler_params=PARAMS,
        name="add_blocks",
    )(parts)


def repeat_kernel(part_ref, out_ref):
    for slot in range(part_ref.shape[0]):
        block = part_ref[slot]
        for i in range(out_ref.shape[0]):
            out_ref[i, slot] = block


def repeat(copies, part):
    return pl.pallas_call(
        repeat_kernel,
        out_shape=jax.ShapeDtypeStruct((copies,) + part.shape, BF16),
        in_specs=[VMEM],
        out_specs=VMEM,
        compiler_params=PARAMS,
        name="repeat",
    )(part)


def add_cells_kernel(parts_ref, out_ref):
    value = parts_ref[0].astype(F32)
    for i in range(1, parts_ref.shape[0]):
        value = value + parts_ref[i].astype(F32)
    total = value.astype(BF16)
    for i in range(out_ref.shape[0]):
        out_ref[i] = total


def add_cells(parts):
    return pl.pallas_call(
        add_cells_kernel,
        out_shape=jax.ShapeDtypeStruct(parts.shape, BF16),
        in_specs=[VMEM],
        out_specs=VMEM,
        compiler_params=PARAMS,
        name="add_cells",
    )(parts)


def eliminate(work, row, column):
    for k in range(work.shape[0]):
        at_row = row[:, 0:1] == k
        at_column = column[0:1, :] == k
        line = work[k : k + 1, :]
        pivot = 1.0 / work[k : k + 1, k : k + 1]
        side = work[:, k : k + 1] - jnp.where(at_row, 1.0, 0.0)
        line = jnp.where(at_column, 1.0, line) * pivot
        kept = jnp.where(at_column, jnp.where(at_row, 1.0, 0.0), work)
        work = kept - side * line
    return work


def solve_into(solve_ref, inverse_ref, gram):
    rank = gram.shape[0]
    row = lax.broadcasted_iota(jnp.int32, (rank, rank), 0)
    column = lax.broadcasted_iota(jnp.int32, (rank, rank), 1)
    diagonal = row == column
    eye = jnp.where(diagonal, 1.0, 0.0)
    matrix = gram + LAMBDA * eye
    along = jnp.where(diagonal, matrix, 0.0)
    down = 1.0 / jnp.sum(along, axis=1, keepdims=True)
    across = 1.0 / jnp.sum(along, axis=0, keepdims=True)
    off = (eye - matrix * across).astype(BF16)
    guess = (eye + (eye - matrix * across)) * down
    guess = guess + dot(guess.astype(BF16), dot(off, off).astype(BF16))
    rest = eye - exact_dot(matrix, guess)
    inverse_ref[...] = guess + split_dot(split(guess), split(rest))
    size = jnp.sum(rest * rest)

    @pl.when(jnp.logical_not(size < 4e-6))
    def _():
        inverse_ref[...] = eliminate(matrix, row, column)

    inverse = inverse_ref[...]
    high, low = split(inverse)
    first, second = split(split_dot((high, low), split(gram)))
    solve_ref[:, 0:rank] = first
    solve_ref[:, rank : 2 * rank] = second
    solve_ref[:, 2 * rank : 3 * rank] = high
    solve_ref[:, 3 * rank : 4 * rank] = low


def second_pass_kernel(
    scale,
    ids_hbm,
    count_ref,
    vals_hbm,
    cell_hbm,
    gene_hbm,
    sums_ref,
    new_hbm,
    out_ref,
    sem,
    out_sem,
    ids_ref,
    pos_ref,
    vals_ref,
    cell_ref,
    gene_ref,
    solve_ref,
    new_ref,
    turned_ref,
    resid_ref,
    total_ref,
):
    blk = vals_ref.shape[1]
    rank = cell_ref.shape[1]
    gene_blocks = gene_ref.shape[0] // blk
    small, values = start_loads(
        sem, [(ids_hbm, ids_ref), (cell_hbm, cell_ref), (gene_hbm, gene_ref)], (vals_hbm, vals_ref.at[: vals_hbm.shape[0]])
    )
    vals_ref[vals_hbm.shape[0]] = jnp.zeros(vals_ref.shape[1:], BF16)
    small[0].wait()
    fill_positions(ids_ref, count_ref, pos_ref)
    halves = [sums_ref[gene_blocks + i].astype(F32) for i in range(2)]
    gram = jnp.concatenate([half[: rank // 2, :] + half[rank // 2 :, :] for half in halves], axis=0)
    solve_into(solve_ref, total_ref.at[:rank, :], gram)
    for copy in small[1:]:
        copy.wait()
    cell_ref[...] = (cell_ref[...].astype(F32) * scale).astype(BF16)
    pairs = gene_blocks // 2
    for pair in range(pairs):
        rows = pl.ds(2 * pair * blk, 2 * blk)
        sums = jnp.concatenate([sums_ref[2 * pair], sums_ref[2 * pair + 1]], axis=1)
        old = gene_ref[rows, :]
        turned = (
            dot(solve_ref[:, 0:rank], old, NT)
            + dot(solve_ref[:, rank : 2 * rank], old, NT)
            + dot(solve_ref[:, 2 * rank : 4 * rank], jnp.concatenate([sums, sums], axis=0))
        )
        new_ref[rows, :] = turned.T.astype(BF16)
        turned_ref[:, rows] = turned.astype(BF16)
    store = pltpu.make_async_copy(new_ref, new_hbm, out_sem)
    store.start()
    gram = dot(turned_ref[...], new_ref[...])
    for copy in values:
        copy.wait()
    for pair in range(pairs):
        genes = new_ref[2 * pair * blk : 2 * (pair + 1) * blk, :]
        residual_pair(vals_ref, pos_ref, resid_ref, dot(cell_ref[...], genes, NT), 2 * pair, gene_blocks, 2 * pair)
    total_ref[...] = dot(resid_ref[...], new_ref[...])
    owners, out_height, _ = out_ref.shape
    count = total_ref.shape[0] // owners
    lines = out_height - count
    for i in range(owners):
        out_ref[i, :count, :] = total_ref[i * count : (i + 1) * count, :].astype(BF16)
        out_ref[i, count:, :] = gram[i * lines : (i + 1) * lines, :].astype(BF16)
    store.wait()


def second_pass(scale, owners, ids, count, values, cells, genes, sums):
    slots, blk, _ = values.shape
    rows, rank = cells.shape
    gene_blocks = genes.shape[0] // blk
    height = (rows + rank) // owners
    return pl.pallas_call(
        functools.partial(second_pass_kernel, scale),
        out_shape=(jax.ShapeDtypeStruct(genes.shape, BF16), jax.ShapeDtypeStruct((owners, height, rank), BF16)),
        in_specs=[HBM, SMEM, HBM, HBM, HBM, VMEM],
        out_specs=(HBM, VMEM),
        scratch_shapes=[
            pltpu.SemaphoreType.DMA((PIECES + 3,)),
            pltpu.SemaphoreType.DMA,
            pltpu.SMEM((slots,), jnp.int32),
            pltpu.SMEM((rows // blk * gene_blocks,), jnp.int32),
            pltpu.VMEM((slots + 1, blk, blk), BF16),
            pltpu.VMEM(cells.shape, BF16),
            pltpu.VMEM(genes.shape, BF16),
            pltpu.VMEM((rank, 4 * rank), BF16),
            pltpu.VMEM(genes.shape, BF16),
            pltpu.VMEM((rank, genes.shape[0]), BF16),
            pltpu.VMEM((rows, genes.shape[0]), BF16),
            pltpu.VMEM((rows, rank), F32),
        ],
        compiler_params=PARAMS,
        name="second_pass",
    )(ids, count, values, cells, genes, sums)


def new_cells_kernel(scale, share, cell_ref, sums_ref, out_ref, solve_ref, gram_ref, inverse_ref):
    rank = cell_ref.shape[1]
    senders, height, _ = sums_ref.shape
    lines = height - share
    for i in range(senders):
        gram_ref[i * lines : (i + 1) * lines, :] = sums_ref[i, share:, :].astype(F32)
    solve_into(solve_ref, inverse_ref, gram_ref[...])
    sums = (sums_ref[:, :share, :].reshape(senders * share, rank).astype(F32) * (1.0 / scale)).astype(BF16)
    out_ref[...] = (
        dot(cell_ref[...], solve_ref[:, 0:rank], NT)
        + dot(cell_ref[...], solve_ref[:, rank : 2 * rank], NT)
        + dot(sums, solve_ref[:, 2 * rank : 3 * rank], NT)
        + dot(sums, solve_ref[:, 3 * rank : 4 * rank], NT)
    ).astype(BF16)


def make_new_cells(scale, share, cells, sums):
    rank = cells.shape[1]
    return pl.pallas_call(
        functools.partial(new_cells_kernel, scale, share),
        out_shape=jax.ShapeDtypeStruct(cells.shape, BF16),
        in_specs=[VMEM] * 2,
        out_specs=VMEM,
        scratch_shapes=[
            pltpu.VMEM((rank, 4 * rank), BF16),
            pltpu.VMEM((rank, rank), F32),
            pltpu.VMEM((rank, rank), F32),
        ],
        compiler_params=PARAMS,
        name="new_cells",
    )(cells, sums)


def exchange(parts, axis, groups=None):
    return lax.all_to_all(parts, axis, 0, 0, tiled=True, axis_index_groups=groups)


def across_cells(blocks):
    owners = blocks.shape[0]
    outer = owners // INNER
    inner_groups = [[o * INNER + i for i in range(INNER)] for o in range(outer)]
    outer_groups = [[o * INNER + i for o in range(outer)] for i in range(INNER)]
    parts = exchange(blocks, "cell", inner_groups).reshape((INNER, outer) + blocks.shape[1:])
    parts = exchange(add_blocks(0, 1, owners - 2, parts)[0], "cell", outer_groups)
    parts = exchange(add_blocks(1, outer, owners - 2, parts[:, None])[:, 0], "cell", outer_groups)
    return exchange(repeat(INNER, parts).reshape(blocks.shape), "cell", inner_groups)


def body(block_values, block_ids, block_count, cell_factor, gene_factor):
    values = block_values[0, 0]
    ids = block_ids[0, 0]
    count = block_count[0]
    rows = cell_factor.shape[0]
    n_cell, n_gene = lax.axis_size("cell"), lax.axis_size("gene")
    scale = (rows * n_cell) ** (-0.5)
    cell_share = rows // n_gene

    sums = across_cells(first_pass(scale, ids, count, values, cell_factor, gene_factor))
    new_genes, cell_terms = second_pass(scale, n_gene, ids, count, values, cell_factor, gene_factor, sums)
    cell_sums = exchange(add_cells(exchange(cell_terms, "gene")), "gene")
    new_cells = make_new_cells(scale, cell_share, cell_factor, cell_sums)
    return new_cells, new_genes


def solution(mesh):
    return jax.shard_map(
        body,
        mesh=mesh,
        in_specs=(
            P("cell", "gene", None, None, None),
            P("cell", "gene", None),
            P("cell", "gene"),
            P("cell", None),
            P("gene", None),
        ),
        out_specs=(P("cell", None), P("gene", None)),
        check_vma=False,
    )
```
